256 devices in a mesh: dp: 64 (over z_hi, x, y, core), mp: 4 (over z_lo).
Axes of the slice: x: 4, y: 4, z: 8 (z_hi: 2, z_lo: 4; z = z_hi * 4 + z_lo), core: 2. Of those that a mesh axis runs over, the one named last changes fastest.
Arguments:
- tokens: bfloat16 [8192, 3072], P('dp', 'mp'), may hold values from -16 to 16
- weight: bfloat16 [3072, 12288], P('dp', 'mp'), may hold values from -0.109375 to 0.109375
- logits: float32 [6, 768, 12288], P(None, 'dp', 'mp'), may hold values from -8 to 320
- gumbel: bfloat16 [6, 768, 12288], P(None, 'dp', 'mp'), may hold values from -2 to 7, as said below
- cotangent: bfloat16 [8192, 12288], P('dp', 'mp'), may hold values from -6 to 6
- moment_one: float32 [6, 768, 12288], P(None, 'dp', 'mp'), may hold values from -6 to 6
- moment_two: float32 [6, 768, 12288], P(None, 'dp', 'mp'), may hold values from 0.01 to 1
Outputs:
- output: bfloat16 [8192, 12288], P('dp', 'mp')
- input_grad: bfloat16 [8192, 3072], P('dp', 'mp')
- new_logits: float32 [6, 768, 12288], P(None, 'dp', 'mp')
- new_moment_one: float32 [6, 768, 12288], P(None, 'dp', 'mp')
- new_moment_two: float32 [6, 768, 12288], P(None, 'dp', 'mp')
The draws below stay inside these ranges and needn't reach their ends.
Inputs may be any that keep to these rules, and one draw needn't show every extreme that they name: `gumbel`: Gumbel(0, 1) noise.
All inputs are finite; a program needn't handle non-finite values.
Results may differ from the reference program's by a relative error of at most 0.002.
The reference program's roundings to bfloat16 on the way (of `masked`) count: a program that leaves them out, or rounds other values in their place, can miss the bound.
Values may be sent and summed in bfloat16 or wider, within the bound.
No kernel may reach another device: no remote copies, remote signals or barrier semaphores. Data moves between devices by JAX's collectives and lax.ppermute only.
A program may use at most 128 MiB of HBM per device.

```python
import math
import jax
import jax.numpy as jnp
import numpy as np
from jax import lax

D = 3072
FF = 12288
PATTERNS = 6
GROUPS = 768
TOKENS = 8192


def draw_logits(key, part):
    key = jax.random.fold_in(key, 11)
    keys = jax.random.split(key, 1)
    shape = (6, D // 4, FF)
    return 2.0 * jnp.clip(jax.random.normal(keys[0], shape, jnp.float32), -4.0, 4.0)


def draw_gumbel(key, part):
    key = jax.random.fold_in(key, 23)
    uniform_draw = jax.random.uniform(key, (6, D // 4, FF), jnp.float32, 0.001, 0.999)
    return (-jnp.log(-jnp.log(uniform_draw))).astype(jnp.bfloat16)


def with_spikes(values, own_key, source, target, blocks, factor):
    def block_of(axis_at):
        return (jnp.arange(values.shape[axis_at]) // (values.shape[axis_at] // blocks)).reshape((-1,) + (1,) * (values.ndim - 1 - axis_at))

    near = jax.random.permutation(own_key, blocks)[block_of(target)]
    second = (block_of(target) + blocks // 2) % blocks
    return jnp.where((block_of(source) == near) | (block_of(source) == second), factor * values, values)


def steps_of(stream_key, shape, shards, least, high):
    factor_of = 1.0
    for position, shards_of in shards:
        heights = jax.random.uniform(jax.random.fold_in(jax.random.fold_in(stream_key, 6), position), (shards_of,), jnp.float32, least / len(shards), high / len(shards))
        factor_of = factor_of * jnp.repeat(jnp.exp(heights), shape[position] // shards_of).reshape((-1,) + (1,) * (len(shape) - 1 - position))
    return factor_of


def gaussian(key, extent, spread, reach, cuts=(), kind=jnp.bfloat16):
    drawn = jax.random.normal(key, extent, jnp.float32) * spread
    if len(cuts) > 0:
        drawn = steps_of(key, extent, cuts, -0.22, 0.18) * drawn
    return jnp.clip(drawn, min=-reach, max=reach).astype(kind)


def bell_draw_with(stream_key, shape, scale, limit, cuts, heavy, held_as=jnp.bfloat16):
    entries = scale * jax.random.normal(stream_key, shape, jnp.float32)
    if cuts:
        entries = entries * steps_of(stream_key, shape, cuts, -0.22, 0.18)
    return jnp.clip(with_spikes(entries, jax.random.fold_in(stream_key, 3), *heavy), -limit, limit).astype(held_as)


def setup_inputs(seed: int = 0) -> dict:
    key_list = jax.random.split(jax.random.key(seed), 8)
    tokens = bell_draw_with(key_list[0], (TOKENS, D), 1.0, 16.0, ((0, 64), (1, 4)), (0, 1, 64, 4.0))
    weight = gaussian(key_list[1], (D, FF), D ** -0.5, 0.109375, ((0, 64), (1, 4)))
    logits = draw_logits(jax.random.fold_in(key_list[7], 71), 0)
    gumbel = draw_gumbel(jax.random.fold_in(key_list[7], 71), 0)
    cotangent = gaussian(key_list[4], (TOKENS, FF), 1.0, 6.0, ((0, 64), (1, 4)))
    moment_one = gaussian(key_list[5], (PATTERNS, GROUPS, FF), 1.0, 6.0, ((1, 64), (2, 4)), jnp.float32)
    moment_two = jnp.clip(jnp.exp(math.log(1.0) - 4.6051702 * jax.random.uniform(key_list[6], (PATTERNS, GROUPS, FF), jnp.float32) ** steps_of(key_list[6], (PATTERNS, GROUPS, FF), ((1, 64), (2, 4)), -0.2, 0.2)), 0.01, 1.0)
    return dict(tokens=tokens, weight=weight, logits=logits, gumbel=gumbel, cotangent=cotangent, moment_one=moment_one, moment_two=moment_two)


beta_one = 0.9
beta_two = 0.999
adam_eps = 1e-08
decay = 0.01
rate = 0.1
adam_step = 10.0

def pattern_table():
    table_rows = []
    for first in range(4):
        for second in range(first + 1, 4):
            table_rows.append([1.0 if k in (first, second) else 0.0 for k in range(4)])
    return np.array(table_rows, np.float32)

def soft_mask(logits, gumbel):
    table = pattern_table()
    scores = logits + gumbel.astype(jnp.float32)
    probs = jax.nn.softmax(scores, axis=0)
    parts = []
    for slot in range(4):
        total = jnp.zeros(probs.shape[1:], jnp.float32)
        for pat in range(6):
            if table[pat, slot] > 0.5:
                total = total + probs[pat]
        parts.append(total)
    mask = jnp.stack(parts, axis=1)
    return (probs, mask)

def logit_update(probs, mgrad, logits, moment_one, moment_two):
    table = pattern_table()
    pieces = []
    for pat in range(6):
        total = jnp.zeros(probs.shape[1:], jnp.float32)
        for slot in range(4):
            if table[pat, slot] > 0.5:
                total = total + mgrad[:, slot, :]
        pieces.append(total)
    pgrad = jnp.stack(pieces, axis=0)
    lgrad = probs * (pgrad - lax.optimization_barrier(jnp.sum(probs * pgrad, axis=0, keepdims=True)))
    new_one = beta_one * moment_one + (1.0 - beta_one) * lgrad
    new_two = beta_two * moment_two + (1.0 - beta_two) * lgrad * lgrad
    first_hat = new_one / (1.0 - beta_one ** adam_step)
    second_hat = new_two / (1.0 - beta_two ** adam_step)
    new_logits = logits - rate * (first_hat / (jnp.sqrt(second_hat) + adam_eps) + decay * logits)
    return (new_logits, new_one, new_two)

def reference(tokens, weight, logits, gumbel, cotangent, moment_one, moment_two):
    probs, mask = soft_mask(logits, gumbel)
    groups = logits.shape[1]
    width = weight.shape[1]
    masked = (weight.astype(jnp.float32) * mask.reshape(4 * groups, width)).astype(jnp.bfloat16)
    output = jnp.dot(tokens, masked, preferred_element_type=jnp.float32).astype(jnp.bfloat16)
    input_grad = lax.dot_general(cotangent, masked, (((1,), (1,)), ((), ())), preferred_element_type=jnp.float32).astype(jnp.bfloat16)
    wgrad = lax.dot_general(tokens, cotangent, (((0,), (0,)), ((), ())), preferred_element_type=jnp.float32)
    mgrad = (weight.astype(jnp.float32) * wgrad).reshape(groups, 4, width)
    new_logits, new_one, new_two = logit_update(probs, mgrad, logits, moment_one, moment_two)
    return (output, input_grad, new_logits, new_one, new_two)
```

```python
import jax
import jax.numpy as jnp
import numpy as np
from jax import lax
from jax.experimental import pallas as pl
from jax.experimental.pallas import tpu as pltpu
from jax.sharding import PartitionSpec as P

beta_one = 0.9
beta_two = 0.999
adam_eps = 1e-08
decay = 0.01
rate = 0.1
adam_step = 10.0

F32 = jnp.float32
BF16 = jnp.bfloat16
AXES = ("dp", "mp")
SIZES = (2, 4, 4, 2, 4)
PAIRS = tuple((i, j) for i in range(4) for j in range(i + 1, 4))
ROWS = 48
HALF = 1536
WIDE = 512
MIB = 1 << 20


def pairs_of(target):
    found = []
    for here in np.ndindex(*SIZES):
        there = tuple(a % b for a, b in zip(target(*here), SIZES))
        found.append(
            (int(np.ravel_multi_index(here, SIZES)), int(np.ravel_multi_index(there, SIZES)))
        )
    return found


def step_a(by):
    return pairs_of(
        lambda z, x, y, c, m: (z, x + by, y, c, m) if c == 0 else (z, x, y + by, c, m)
    )


def step_b(by):
    return pairs_of(
        lambda z, x, y, c, m: (z, x, y + by, c, m) if c == 0 else (z, x + by, y, c, m)
    )


SIBLING = pairs_of(lambda z, x, y, c, m: (z, x, y, c + 1, m))
PARTNER = pairs_of(lambda z, x, y, c, m: (z + 1, x, y, c, m))
A_UP, A_DOWN = step_a(1), step_a(-1)
B_UP, B_DOWN = step_b(1), step_b(-1)


def around(by):
    return pairs_of(lambda z, x, y, c, m: (z, x, y, c, m + by))


def send(value, pairs):
    return lax.ppermute(value, AXES, pairs)


def dot(a, b, dims):
    return lax.dot_general(a, b, (dims, ((), ())), preferred_element_type=F32)


def mask_kernel(logits, gumbel, weight, probs, masked, spread):
    scores = [logits[p] + gumbel[p].astype(F32) for p in range(6)]
    top = scores[0]
    for p in range(1, 6):
        top = jnp.maximum(top, scores[p])
    exps = [jnp.exp(s - top) for s in scores]
    total = exps[0]
    for p in range(1, 6):
        total = total + exps[p]
    share = [e / total for e in exps]
    for p in range(6):
        probs[p] = share[p]
    for slot in range(4):
        kept = [share[p] for p in range(6) if slot in PAIRS[p]]
        mask = kept[0] + kept[1] + kept[2]
        for j in range(WIDE // 128):
            at = j * 128
            spread[pl.ds(j * ROWS + slot, 12, stride=4), :] = mask[:, at : at + 128]
    for j in range(WIDE // 128):
        at = j * 128
        part = weight[:, at : at + 128].astype(F32) * spread[j * ROWS : (j + 1) * ROWS, :]
        masked[:, at : at + 128] = part.astype(BF16)


def make_masked(logits, gumbel, weight):
    cols = weight.shape[1]
    wide = WIDE
    three = pl.BlockSpec((6, 12, wide), lambda i: (0, 0, i))
    two = pl.BlockSpec((ROWS, wide), lambda i: (0, i))
    return pl.pallas_call(
        mask_kernel,
        grid=(cols // wide,),
        in_specs=[three, three, two],
        out_specs=[three, two],
        out_shape=[
            jax.ShapeDtypeStruct((6, 12, cols), F32),
            jax.ShapeDtypeStruct((ROWS, cols), BF16),
        ],
        scratch_shapes=[pltpu.VMEM((wide // 128 * ROWS, 128), F32)],
        compiler_params=pltpu.CompilerParams(vmem_limit_bytes=16 * MIB),
        cost_estimate=pl.CostEstimate(flops=8000000, bytes_accessed=2800000, transcendentals=221184),
    )(logits, gumbel, weight)


def adam_kernel(wgrad, weight, probs, logits, one, two, new_logits, new_one, new_two, spread):
    for j in range(WIDE // 128):
        at = j * 128
        spread[j * ROWS : (j + 1) * ROWS, :] = (
            weight[:, at : at + 128].astype(F32) * wgrad[:, at : at + 128]
        )
    slots = [
        jnp.concatenate(
            [spread[pl.ds(j * ROWS + slot, 12, stride=4), :] for j in range(WIDE // 128)], axis=1
        )
        for slot in range(4)
    ]
    pgrad = [slots[i] + slots[j] for i, j in PAIRS]
    share = [probs[p] for p in range(6)]
    mean = share[0] * pgrad[0]
    for p in range(1, 6):
        mean = mean + share[p] * pgrad[p]
    for p in range(6):
        lgrad = share[p] * (pgrad[p] - mean)
        first = beta_one * one[p] + (1.0 - beta_one) * lgrad
        second = beta_two * two[p] + (1.0 - beta_two) * lgrad * lgrad
        new_one[p] = first
        new_two[p] = second
        first_hat = first / (1.0 - beta_one**adam_step)
        second_hat = second / (1.0 - beta_two**adam_step)
        old = logits[p]
        new_logits[p] = old - rate * (first_hat / (jnp.sqrt(second_hat) + adam_eps) + decay * old)


def adam(wgrad, weight, probs, logits, one, two):
    cols = weight.shape[1]
    wide = WIDE
    three = pl.BlockSpec((6, 12, wide), lambda i: (0, 0, i))
    flat = pl.BlockSpec((ROWS, wide), lambda i: (0, i))
    out = jax.ShapeDtypeStruct((6, 12, cols), F32)
    return pl.pallas_call(
        adam_kernel,
        grid=(cols // wide,),
        in_specs=[flat, flat, three, three, three, three],
        out_specs=[three, three, three],
        out_shape=[out, out, out],
        scratch_shapes=[pltpu.VMEM((wide // 128 * ROWS, 128), F32)],
        compiler_params=pltpu.CompilerParams(vmem_limit_bytes=16 * MIB),
        cost_estimate=pl.CostEstimate(flops=8000000, bytes_accessed=7000000, transcendentals=221184),
    )(wgrad, weight, probs, logits, one, two)


def meet_kernel(place, *refs):
    out = refs[-1]
    for side in range(2):
        for r in range(4):
            source = refs[side * 4 + r]
            for i in range(16):
                at = pl.multiple_of(place[r * 16 + i] * ROWS, ROWS)
                out[pl.ds(at, ROWS), side * 128 : side * 128 + 128] = source[
                    i * ROWS : (i + 1) * ROWS, :
                ]


def meet(place, parts):
    return pl.pallas_call(
        meet_kernel,
        in_specs=[pl.BlockSpec(memory_space=pltpu.SMEM)]
        + [pl.BlockSpec(memory_space=pltpu.VMEM)] * 8,
        out_specs=pl.BlockSpec(memory_space=pltpu.VMEM),
        out_shape=jax.ShapeDtypeStruct((3072, 256), BF16),
        compiler_params=pltpu.CompilerParams(vmem_limit_bytes=16 * MIB),
        cost_estimate=pl.CostEstimate(flops=0, bytes_accessed=3200000, transcendentals=0),
    )(place, *parts)


def part_kernel(place, *refs):
    mine, other = refs[-2:]
    for piece in range(16):
        for i in range(4):
            at = pl.multiple_of(place[piece * 4 + i] * ROWS, ROWS)
            mine[pl.ds(at, ROWS), :] = refs[piece][i * ROWS : (i + 1) * ROWS, :128]
            other[pl.ds(at, ROWS), :] = refs[piece][i * ROWS : (i + 1) * ROWS, 128:]


def part(place, pieces):
    out = jax.ShapeDtypeStruct((3072, 128), F32)
    return pl.pallas_call(
        part_kernel,
        in_specs=[pl.BlockSpec(memory_space=pltpu.SMEM)]
        + [pl.BlockSpec(memory_space=pltpu.VMEM)] * 16,
        out_specs=[pl.BlockSpec(memory_space=pltpu.VMEM)] * 2,
        out_shape=[out, out],
        compiler_params=pltpu.CompilerParams(vmem_limit_bytes=16 * MIB),
        cost_estimate=pl.CostEstimate(flops=0, bytes_accessed=6400000, transcendentals=0),
    )(place, *pieces)


def local(tokens, weight, logits, gumbel, cotangent, moment_one, moment_two):
    dp = lax.axis_index("dp")
    mp = lax.axis_index("mp")
    core, y, x, zh = dp % 2, (dp // 2) % 4, (dp // 8) % 4, dp // 32

    def half(value, which):
        return lax.dynamic_slice_in_dim(value, which * HALF, HALF, axis=1)

    whole = np.arange(64)
    dx, dy = (whole // 8 - x) % 4, (whole // 2 - y) % 4
    da, db = jnp.where(core == 0, dx, dy), jnp.where(core == 0, dy, dx)
    met_at = ((((whole // 32) ^ zh) * 4 + db) * 4 + da) * 2 + ((whole % 2) ^ core)
    met_at = met_at.astype(jnp.int32)
    order = np.arange(64)
    oz, ob, oa, oc = order // 32, (order // 8) % 4, (order // 2) % 4, order % 2
    ox, oy = jnp.where(core == 0, oa, ob), jnp.where(core == 0, ob, oa)
    lies_at = (((oz ^ zh) * 4 + (ox + x) % 4) * 4 + (oy + y) % 4) * 2 + (oc ^ core)
    lies_at = lies_at.astype(jnp.int32)

    probs, masked = make_masked(logits, gumbel, weight)
    block = jnp.concatenate([half(masked, core), send(half(masked, 1 - core), SIBLING)], axis=0)
    blocks = [block, send(block, PARTNER)]

    flipped = tokens.T
    own = [flipped] + [send(flipped, around(r)) for r in (1, 2, 3)]
    others = [send(v, SIBLING) for v in own]
    came = jnp.concatenate([((mp - r) % 4) * 16 + np.arange(16) for r in range(4)])
    acts = meet(met_at[came], own + others)
    cot = jnp.concatenate(
        [half(cotangent, core), send(half(cotangent, 1 - core), SIBLING)], axis=0
    )

    def rows_of(dz, db, upper):
        start = ((dz * 4 + db) * 2 + upper) * 192
        return acts[start : start + 192]

    pieces = {}
    for dz in range(2):
        b0 = blocks[dz]
        b1 = send(b0, A_DOWN)
        b3 = send(b0, A_UP)
        b2 = [send(b1[:ROWS], A_DOWN), send(b3[ROWS:], A_UP)]
        low = jnp.concatenate([b0, b1], axis=0)
        high = jnp.concatenate(b2 + [b3], axis=0)
        pieces[dz, 0] = (low, high)
        low1, low3 = send(low, B_DOWN), send(low, B_UP)
        high1, high3 = send(high, B_DOWN), send(high, B_UP)
        pieces[dz, 1] = (low1, high1)
        pieces[dz, 3] = (low3, high3)
        pieces[dz, 2] = (send(low1, B_DOWN), send(high3, B_UP))

    def share(dz, db, upper):
        return dot(rows_of(dz, db, upper), cot, ((1,), (0,)))

    sums = {}
    for dz in (1, 0):
        low2 = send(share(dz, 2, 0).astype(BF16), B_UP)
        high2 = send(share(dz, 2, 1).astype(BF16), B_DOWN)
        high1 = send(share(dz, 1, 1).astype(BF16), B_UP)
        low3 = send(share(dz, 3, 0).astype(BF16), B_DOWN)
        low1 = send((share(dz, 1, 0) + low2.astype(F32)).astype(BF16), B_UP)
        high3 = send((share(dz, 3, 1) + high2.astype(F32)).astype(BF16), B_DOWN)
        low = share(dz, 0, 0) + low1.astype(F32) + low3.astype(F32)
        high = share(dz, 0, 1) + high1.astype(F32) + high3.astype(F32)
        a0, a1, a2, a3 = low[:96], low[96:], high[:96], high[96:]
        c2 = send(a2[:ROWS].astype(BF16), A_UP)
        d2 = send(a2[ROWS:].astype(BF16), A_DOWN)
        c1 = jnp.concatenate([a1[:ROWS] + c2.astype(F32), a1[ROWS:]], axis=0)
        d3 = jnp.concatenate([a3[:ROWS], a3[ROWS:] + d2.astype(F32)], axis=0)
        c1 = send(c1.astype(BF16), A_UP)
        d3 = send(d3.astype(BF16), A_DOWN)
        sums[dz] = a0 + c1.astype(F32) + d3.astype(F32)
    wsum = sums[0] + send(sums[1].astype(BF16), PARTNER).astype(F32)
    other = send(wsum[ROWS:], SIBLING)
    wgrad = jnp.where(
        core == 0,
        jnp.concatenate([wsum[:ROWS], other], axis=1),
        jnp.concatenate([other, wsum[:ROWS]], axis=1),
    )
    new_logits, new_one, new_two = adam(wgrad, weight, probs, logits, moment_one, moment_two)

    result = None
    grads = []
    for dz in range(2):
        for db in range(4):
            for upper in range(2):
                piece = pieces[dz, db][upper]
                term = dot(rows_of(dz, db, upper), piece, ((0,), (0,)))
                result = term if result is None else result + term
                grads.append(dot(piece, cot, ((1,), (1,))))
    result = result.astype(BF16)
    other = send(result[128:], SIBLING)
    output = jnp.where(
        core == 0,
        jnp.concatenate([result[:128], other], axis=1),
        jnp.concatenate([other, result[:128]], axis=1),
    )

    mine, theirs = part(lies_at, grads)
    grad = mine + send(theirs, SIBLING)

    def quarter(r):
        return lax.dynamic_slice_in_dim(grad, ((mp + r) % 4) * 768, 768, axis=0)

    total = quarter(0)
    for r in (1, 2, 3):
        total = total + send(quarter(r), around(r))
    input_grad = total.astype(BF16).T
    return (output, input_grad, new_logits, new_one, new_two)


def solution(mesh):
    placed = (
        P("dp", "mp"),
        P("dp", "mp"),
        P(None, "dp", "mp"),
        P(None, "dp", "mp"),
        P("dp", "mp"),
        P(None, "dp", "mp"),
        P(None, "dp", "mp"),
    )
    return jax.shard_map(
        local,
        mesh=mesh,
        in_specs=placed,
        out_specs=(
            P("dp", "mp"),
            P("dp", "mp"),
            P(None, "dp", "mp"),
            P(None, "dp", "mp"),
            P(None, "dp", "mp"),
        ),
        check_vma=False,
    )
```

```python
import functools
import math

import jax
import jax.numpy as jnp
import numpy as np
from jax import lax
from jax.experimental import pallas as pl
from jax.experimental.pallas import tpu as pltpu
from jax.sharding import PartitionSpec as P

beta_one = 0.9
beta_two = 0.999
adam_eps = 1e-08
decay = 0.01
rate = 0.1
adam_step = 10.0

F32 = jnp.float32
BF16 = jnp.bfloat16
AXES = ("dp", "mp")
SIZES = (2, 4, 4, 2, 4)
PAIRS = tuple((i, j) for i in range(4) for j in range(i + 1, 4))
ROWS = 48
HALF = 1536
WIDE = 512
TILE = 512
MIB = 1 << 20
IN_VMEM = pl.BlockSpec(memory_space=pltpu.VMEM)


def pairs_of(target):
    found = []
    for here in np.ndindex(*SIZES):
        there = tuple(a % b for a, b in zip(target(*here), SIZES))
        found.append(
            (int(np.ravel_multi_index(here, SIZES)), int(np.ravel_multi_index(there, SIZES)))
        )
    return found


def step_a(by):
    return pairs_of(
        lambda z, x, y, c, m: (z, x + by, y, c, m) if c == 0 else (z, x, y + by, c, m)
    )


def step_b(by):
    return pairs_of(
        lambda z, x, y, c, m: (z, x, y + by, c, m) if c == 0 else (z, x + by, y, c, m)
    )


SIBLING = pairs_of(lambda z, x, y, c, m: (z, x, y, c + 1, m))
PARTNER = pairs_of(lambda z, x, y, c, m: (z + 1, x, y, c, m))
A_UP, A_DOWN, A_TWO = step_a(1), step_a(-1), step_a(2)
B_UP, B_DOWN = step_b(1), step_b(-1)


def around(by):
    return pairs_of(lambda z, x, y, c, m: (z, x, y, c, m + by))


def send(value, pairs):
    return lax.ppermute(value, AXES, pairs)


def dot(a, b, dims):
    return lax.dot_general(a, b, (dims, ((), ())), preferred_element_type=F32)


def mask_kernel(logits, gumbel, weight, probs, masked, spread):
    scores = [logits[p] + gumbel[p].astype(F32) for p in range(6)]
    top = scores[0]
    for p in range(1, 6):
        top = jnp.maximum(top, scores[p])
    exps = [jnp.exp(s - top) for s in scores]
    total = exps[0]
    for p in range(1, 6):
        total = total + exps[p]
    share = [e / total for e in exps]
    for p in range(6):
        probs[p] = share[p]
    for slot in range(4):
        kept = [share[p] for p in range(6) if slot in PAIRS[p]]
        mask = kept[0] + kept[1] + kept[2]
        for j in range(WIDE // 128):
            at = j * 128
            spread[pl.ds(j * ROWS + slot, 12, stride=4), :] = mask[:, at : at + 128]
    for j in range(WIDE // 128):
        at = j * 128
        part = weight[:, at : at + 128].astype(F32) * spread[j * ROWS : (j + 1) * ROWS, :]
        masked[:, at : at + 128] = part.astype(BF16)


def make_masked(logits, gumbel, weight):
    cols = weight.shape[1]
    wide = WIDE
    three = pl.BlockSpec((6, 12, wide), lambda i: (0, 0, i))
    two = pl.BlockSpec((ROWS, wide), lambda i: (0, i))
    return pl.pallas_call(
        mask_kernel,
        grid=(cols // wide,),
        in_specs=[three, three, two],
        out_specs=[three, two],
        out_shape=[
            jax.ShapeDtypeStruct((6, 12, cols), F32),
            jax.ShapeDtypeStruct((ROWS, cols), BF16),
        ],
        scratch_shapes=[pltpu.VMEM((wide // 128 * ROWS, 128), F32)],
        compiler_params=pltpu.CompilerParams(vmem_limit_bytes=16 * MIB),
        cost_estimate=pl.CostEstimate(flops=8000000, bytes_accessed=2800000, transcendentals=221184),
    )(logits, gumbel, weight)


def adam_kernel(wgrad, weight, probs, logits, one, two, new_logits, new_one, new_two, spread):
    for j in range(WIDE // 128):
        at = j * 128
        spread[j * ROWS : (j + 1) * ROWS, :] = (
            weight[:, at : at + 128].astype(F32) * wgrad[:, at : at + 128]
        )
    slots = [
        jnp.concatenate(
            [spread[pl.ds(j * ROWS + slot, 12, stride=4), :] for j in range(WIDE // 128)], axis=1
        )
        for slot in range(4)
    ]
    pgrad = [slots[i] + slots[j] for i, j in PAIRS]
    share = [probs[p] for p in range(6)]
    mean = share[0] * pgrad[0]
    for p in range(1, 6):
        mean = mean + share[p] * pgrad[p]
    for p in range(6):
        lgrad = share[p] * (pgrad[p] - mean)
        first = beta_one * one[p] + (1.0 - beta_one) * lgrad
        second = beta_two * two[p] + (1.0 - beta_two) * lgrad * lgrad
        new_one[p] = first
        new_two[p] = second
        first_hat = first / (1.0 - beta_one**adam_step)
        second_hat = second / (1.0 - beta_two**adam_step)
        old = logits[p]
        new_logits[p] = old - rate * (first_hat / (jnp.sqrt(second_hat) + adam_eps) + decay * old)


def adam(wgrad, weight, probs, logits, one, two):
    cols = weight.shape[1]
    wide = WIDE
    three = pl.BlockSpec((6, 12, wide), lambda i: (0, 0, i))
    flat = pl.BlockSpec((ROWS, wide), lambda i: (0, i))
    out = jax.ShapeDtypeStruct((6, 12, cols), F32)
    return pl.pallas_call(
        adam_kernel,
        grid=(cols // wide,),
        in_specs=[flat, flat, three, three, three, three],
        out_specs=[three, three, three],
        out_shape=[out, out, out],
        scratch_shapes=[pltpu.VMEM((wide // 128 * ROWS, 128), F32)],
        compiler_params=pltpu.CompilerParams(vmem_limit_bytes=16 * MIB),
        cost_estimate=pl.CostEstimate(flops=8000000, bytes_accessed=7000000, transcendentals=221184),
    )(wgrad, weight, probs, logits, one, two)


def meet_kernel(place, mine, other, out):
    for i in range(64):
        at = pl.multiple_of(place[i] * ROWS, ROWS)
        out[pl.ds(at, ROWS), :128] = mine[i * ROWS : (i + 1) * ROWS, :]
        out[pl.ds(at, ROWS), 128:] = other[i * ROWS : (i + 1) * ROWS, :]


def meet(place, mine, other):
    return pl.pallas_call(
        meet_kernel,
        in_specs=[pl.BlockSpec(memory_space=pltpu.SMEM)] + [IN_VMEM] * 2,
        out_specs=IN_VMEM,
        out_shape=jax.ShapeDtypeStruct((3072, 256), BF16),
        compiler_params=pltpu.CompilerParams(vmem_limit_bytes=16 * MIB),
        cost_estimate=pl.CostEstimate(flops=0, bytes_accessed=3200000, transcendentals=0),
    )(place, mine, other)


def part_kernel(place, *refs):
    mine, other = refs[-2:]
    at_block = 0
    for ref in refs[:-2]:
        for i in range(ref.shape[0] // ROWS):
            at = pl.multiple_of(place[at_block] * ROWS, ROWS)
            mine[pl.ds(at, ROWS), :] = ref[i * ROWS : (i + 1) * ROWS, :128]
            other[pl.ds(at, ROWS), :] = ref[i * ROWS : (i + 1) * ROWS, 128:]
            at_block += 1


def part(place, pieces):
    out = jax.ShapeDtypeStruct((3072, 128), F32)
    return pl.pallas_call(
        part_kernel,
        in_specs=[pl.BlockSpec(memory_space=pltpu.SMEM)] + [IN_VMEM] * len(pieces),
        out_specs=[IN_VMEM] * 2,
        out_shape=[out, out],
        compiler_params=pltpu.CompilerParams(vmem_limit_bytes=16 * MIB),
        cost_estimate=pl.CostEstimate(flops=0, bytes_accessed=6400000, transcendentals=0),
    )(place, *pieces)


def share(acts, cot, start, count, at):
    return dot(acts[start : start + count, :], cot[:, at : at + TILE], ((1,), (0,)))


def line_kernel(*refs):
    out = refs[-1]
    for i, ref in enumerate(refs[:-1]):
        out[i * 96 : (i + 1) * 96, :] = ref[...]


def lead_kernel(start, acts, cot, near, far, up, down):
    up[:192, :] = far[192:384, :]
    down[:192, :] = near[:192, :]
    for at in range(0, HALF, TILE):
        cols = slice(at, at + TILE)
        up[192:, cols] = share(acts, cot, start, 192, at).astype(BF16)
        down[192:, cols] = share(acts, cot, start + 192, 192, at).astype(BF16)


def follow_kernel(start_up, start_down, acts, cot, low, high, *refs):
    up, down = refs[-2:]
    base = 96 * (len(refs) - 2)
    for i, ref in enumerate(refs[:-2]):
        up[i * 96 : (i + 1) * 96, :] = ref[...]
        down[i * 96 : (i + 1) * 96, :] = ref[...]
    for at in range(0, HALF, TILE):
        cols = slice(at, at + TILE)
        got = share(acts, cot, start_up, 192, at) + low[192:, cols].astype(F32)
        up[base : base + 192, cols] = got.astype(BF16)
        up[base + 192 :, cols] = share(acts, cot, start_up + 192, 192, at).astype(BF16)
        down[base : base + 192, cols] = share(acts, cot, start_down, 192, at).astype(BF16)
        got = share(acts, cot, start_down + 192, 192, at) + high[192:, cols].astype(F32)
        down[base + 192 :, cols] = got.astype(BF16)


def keep_kernel(start, acts, cot, up, down, own, *others):
    base = up.shape[0] - 384
    for at in range(0, HALF, TILE):
        cols = slice(at, at + TILE)
        for i in range(4):
            rows = slice(base + i * 96, base + i * 96 + 96)
            got = share(acts, cot, start + i * 96, 96, at)
            got = got + up[rows, cols].astype(F32) + down[rows, cols].astype(F32)
            if i == 0:
                own[:, cols] = got
            else:
                others[i - 1][:, cols] = got.astype(BF16)


def in_vmem(kernel, out_shape, flops, *args):
    moved = sum(a.size * a.dtype.itemsize for a in args)
    moved += sum(math.prod(o.shape) * o.dtype.itemsize for o in out_shape)
    return pl.pallas_call(
        kernel,
        in_specs=[IN_VMEM] * len(args),
        out_specs=[IN_VMEM] * len(out_shape),
        out_shape=out_shape,
        compiler_params=pltpu.CompilerParams(vmem_limit_bytes=24 * MIB),
        cost_estimate=pl.CostEstimate(flops=flops, bytes_accessed=moved, transcendentals=0),
    )(*args)


def shape16(rows):
    return jax.ShapeDtypeStruct((rows, HALF), BF16)


def product_kernel(starts, counts, first, acts, cot, *refs):
    size = len(starts)
    before = None if first else refs[0]
    refs = refs if first else refs[1:]
    pieces, result, grads = refs[:size], refs[size], refs[size + 1 :]
    for at in range(0, HALF, TILE):
        cols = slice(at, at + TILE)
        total = None if first else before[:, cols]
        for start, count, piece in zip(starts, counts, pieces):
            term = dot(acts[start : start + count, :], piece[:count, cols], ((0,), (0,)))
            total = term if total is None else total + term
        result[:, cols] = total
    for count, piece, grad in zip(counts, pieces, grads):
        grad[...] = dot(piece[:count, :], cot[...], ((1,), (1,)))


def products(acts, cot, before, starts, counts, pieces):
    first = before is None
    shapes = [jax.ShapeDtypeStruct((256, HALF), F32)]
    shapes += [jax.ShapeDtypeStruct((n, 256), F32) for n in counts]
    args = [acts, cot] + ([] if first else [before]) + pieces
    return in_vmem(
        functools.partial(product_kernel, starts, counts, first),
        shapes, 4 * sum(counts) * 256 * HALF, *args
    )


def local(tokens, weight, logits, gumbel, cotangent, moment_one, moment_two):
    dp = lax.axis_index("dp")
    mp = lax.axis_index("mp")
    core, y, x, zh = dp % 2, (dp // 2) % 4, (dp // 8) % 4, dp // 32

    def half(value, which):
        return lax.dynamic_slice_in_dim(value, which * HALF, HALF, axis=1)

    whole = np.arange(64)
    dx, dy = (whole // 8 - x) % 4, (whole // 2 - y) % 4
    da, db = jnp.where(core == 0, dx, dy), jnp.where(core == 0, dy, dx)
    met_at = ((((whole // 32) ^ zh) * 4 + db) * 4 + da) * 2 + ((whole % 2) ^ core)
    met_at = met_at.astype(jnp.int32)
    order = np.arange(64)
    oz, ob, oa, oc = order // 32, (order // 8) % 4, (order // 2) % 4, order % 2
    ox, oy = jnp.where(core == 0, oa, ob), jnp.where(core == 0, ob, oa)
    lies_at = (((oz ^ zh) * 4 + (ox + x) % 4) * 4 + (oy + y) % 4) * 2 + (oc ^ core)
    lies_at = lies_at.astype(jnp.int32)

    probs, masked = make_masked(logits, gumbel, weight)
    block = jnp.concatenate([half(masked, core), send(half(masked, 1 - core), SIBLING)], axis=0)
    blocks = [block, send(block, PARTNER)]

    flipped = tokens.T
    own = jnp.concatenate([flipped] + [send(flipped, around(r)) for r in (1, 2, 3)], axis=0)
    others = send(own, SIBLING)
    came = jnp.concatenate([((mp - r) % 4) * 16 + np.arange(16) for r in range(4)])
    acts = meet(met_at[came], own, others)
    cot = jnp.concatenate(
        [half(cotangent, core), send(half(cotangent, 1 - core), SIBLING)], axis=0
    )

    def start_of(dz, db):
        return (dz * 4 + db) * 384

    def spread_a(mine):
        return [mine, send(mine, A_DOWN), send(mine, A_TWO), send(mine, A_UP)]

    def kept(dz, up, down):
        own, one, two, three = in_vmem(
            functools.partial(keep_kernel, start_of(dz, 0)),
            [jax.ShapeDtypeStruct((96, HALF), F32)] + [shape16(96)] * 3, work, acts, cot, up, down,
        )
        one, two, three = send(one, A_UP), send(two, A_TWO), send(three, A_DOWN)
        return own + one.astype(F32) + two.astype(F32) + three.astype(F32)

    work = 2 * 384 * 256 * HALF
    line0 = in_vmem(line_kernel, [shape16(384)], 0, *spread_a(blocks[0]))[0]
    near0, far0 = send(line0, B_DOWN), send(line0, B_UP)
    up, down = in_vmem(
        functools.partial(lead_kernel, start_of(1, 2)), [shape16(384)] * 2, work, acts, cot, near0, far0
    )
    high0, low0 = send(up, B_UP), send(down, B_DOWN)
    line1, down = in_vmem(
        functools.partial(follow_kernel, start_of(1, 1), start_of(1, 3)),
        [shape16(768)] * 2, 2 * work, acts, cot, high0, low0, *spread_a(blocks[1]),
    )
    far1, near1 = send(line1, B_UP), send(down, B_DOWN)
    up, down = in_vmem(
        functools.partial(lead_kernel, start_of(0, 2)), [shape16(384)] * 2, work, acts, cot, near1, far1
    )
    high1, low1 = send(up, B_UP), send(down, B_DOWN)
    sums = {1: kept(1, far1, near1)}
    up, down = in_vmem(
        functools.partial(follow_kernel, start_of(0, 1), start_of(0, 3)),
        [shape16(384)] * 2, 2 * work, acts, cot, high1, low1,
    )
    up, down = send(up, B_UP), send(down, B_DOWN)
    sums[0] = kept(0, up, down)
    wsum = sums[0] + send(sums[1].astype(BF16), PARTNER).astype(F32)
    other = send(wsum[ROWS:], SIBLING)
    wgrad = jnp.where(
        core == 0,
        jnp.concatenate([wsum[:ROWS], other], axis=1),
        jnp.concatenate([other, wsum[:ROWS]], axis=1),
    )
    new_logits, new_one, new_two = adam(wgrad, weight, probs, logits, moment_one, moment_two)

    near = [start_of(dz, db) for dz in range(2) for db in (0, 1, 3)]
    opposite = [(start_of(dz, 2), start_of(dz, 2) + 192) for dz in range(2)]
    result, g0, g1, g3, g2, g4 = products(
        acts, cot, None, near[:3] + list(opposite[0]), [384] * 3 + [192] * 2,
        [line0, near0, far0, low0, high0],
    )
    result, h0, h1, h3 = products(
        acts, cot, result, near[3:], [384] * 3, [line1, near1, far1]
    )
    result, h2, h4 = products(acts, cot, result, opposite[1], [192] * 2, [low1, high1])
    grads = [g0, g1, g2, g4, g3, h0, h1, h2, h4, h3]
    result = result.astype(BF16)
    other = send(result[128:], SIBLING)
    output = jnp.where(
        core == 0,
        jnp.concatenate([result[:128], other], axis=1),
        jnp.concatenate([other, result[:128]], axis=1),
    )

    mine, theirs = part(lies_at, grads)
    grad = mine + send(theirs, SIBLING)

    def quarter(r):
        return lax.dynamic_slice_in_dim(grad, ((mp + r) % 4) * 768, 768, axis=0)

    total = quarter(0)
    for r in (1, 2, 3):
        total = total + send(quarter(r), around(r))
    input_grad = total.astype(BF16).T
    return (output, input_grad, new_logits, new_one, new_two)


def solution(mesh):
    placed = (
        P("dp", "mp"),
        P("dp", "mp"),
        P(None, "dp", "mp"),
        P(None, "dp", "mp"),
        P("dp", "mp"),
        P(None, "dp", "mp"),
        P(None, "dp", "mp"),
    )
    return jax.shard_map(
        local,
        mesh=mesh,
        in_specs=placed,
        out_specs=(
            P("dp", "mp"),
            P("dp", "mp"),
            P(None, "dp", "mp"),
            P(None, "dp", "mp"),
            P(None, "dp", "mp"),
        ),
        check_vma=False,
    )
```

```python
import functools

import jax
import jax.numpy as jnp
import numpy as np
from jax import lax
from jax.experimental import pallas as pl
from jax.experimental.pallas import tpu as pltpu
from jax.sharding import PartitionSpec as P

beta_one = 0.9
beta_two = 0.999
adam_eps = 1e-08
decay = 0.01
rate = 0.1
adam_step = 10.0

F32 = jnp.float32
BF16 = jnp.bfloat16
AXES = ("dp", "mp")
SIZES = (2, 4, 4, 2, 4)
PAIRS = tuple((i, j) for i in range(4) for j in range(i + 1, 4))
ROWS = 48
HALF = 1536
WIDE = 512
TILE = 512
MIB = 1 << 20
IN_VMEM = pl.BlockSpec(memory_space=pltpu.VMEM)
LIGHT = pl.CostEstimate(flops=0, bytes_accessed=1, transcendentals=0)


def pairs_of(target):
    found = []
    for here in np.ndindex(*SIZES):
        there = tuple(a % b for a, b in zip(target(*here), SIZES))
        found.append(
            (int(np.ravel_multi_index(here, SIZES)), int(np.ravel_multi_index(there, SIZES)))
        )
    return found


def step_a(by):
    return pairs_of(
        lambda z, x, y, c, m: (z, x + by, y, c, m) if c == 0 else (z, x, y + by, c, m)
    )


def step_b(by):
    return pairs_of(
        lambda z, x, y, c, m: (z, x, y + by, c, m) if c == 0 else (z, x + by, y, c, m)
    )


SIBLING = pairs_of(lambda z, x, y, c, m: (z, x, y, c + 1, m))
PARTNER = pairs_of(lambda z, x, y, c, m: (z + 1, x, y, c, m))
A_UP, A_DOWN, A_TWO = step_a(1), step_a(-1), step_a(2)
B_UP, B_DOWN = step_b(1), step_b(-1)


def around(by):
    return pairs_of(lambda z, x, y, c, m: (z, x, y, c, m + by))


def crossed(by):
    return pairs_of(lambda z, x, y, c, m: (z, x, y, c, m ^ by))


def send(value, pairs):
    return lax.ppermute(value, AXES, pairs)


def dot(a, b, dims):
    return lax.dot_general(a, b, (dims, ((), ())), preferred_element_type=F32)


def mask_kernel(logits, gumbel, weight, probs, masked, spread):
    scores = [logits[p] + gumbel[p].astype(F32) for p in range(6)]
    top = scores[0]
    for p in range(1, 6):
        top = jnp.maximum(top, scores[p])
    exps = [jnp.exp(s - top) for s in scores]
    total = exps[0]
    for p in range(1, 6):
        total = total + exps[p]
    share = [e / total for e in exps]
    for p in range(6):
        probs[p] = share[p]
    for slot in range(4):
        kept = [share[p] for p in range(6) if slot in PAIRS[p]]
        mask = kept[0] + kept[1] + kept[2]
        for j in range(WIDE // 128):
            at = j * 128
            spread[pl.ds(j * ROWS + slot, 12, stride=4), :] = mask[:, at : at + 128]
    for j in range(WIDE // 128):
        at = j * 128
        part = weight[:, at : at + 128].astype(F32) * spread[j * ROWS : (j + 1) * ROWS, :]
        masked[:, at : at + 128] = part.astype(BF16)


def make_masked(logits, gumbel, weight):
    cols = weight.shape[1]
    wide = WIDE
    three = pl.BlockSpec((6, 12, wide), lambda i: (0, 0, i))
    two = pl.BlockSpec((ROWS, wide), lambda i: (0, i))
    return pl.pallas_call(
        mask_kernel,
        grid=(cols // wide,),
        in_specs=[three, three, two],
        out_specs=[three, two],
        out_shape=[
            jax.ShapeDtypeStruct((6, 12, cols), F32),
            jax.ShapeDtypeStruct((ROWS, cols), BF16),
        ],
        scratch_shapes=[pltpu.VMEM((wide // 128 * ROWS, 128), F32)],
        compiler_params=pltpu.CompilerParams(vmem_limit_bytes=16 * MIB),
        cost_estimate=LIGHT,
    )(logits, gumbel, weight)


def adam_kernel(wgrad, weight, probs, logits, one, two, new_logits, new_one, new_two, spread):
    for j in range(WIDE // 128):
        at = j * 128
        spread[j * ROWS : (j + 1) * ROWS, :] = (
            weight[:, at : at + 128].astype(F32) * wgrad[:, at : at + 128]
        )
    slots = [
        jnp.concatenate(
            [spread[pl.ds(j * ROWS + slot, 12, stride=4), :] for j in range(WIDE // 128)], axis=1
        )
        for slot in range(4)
    ]
    pgrad = [slots[i] + slots[j] for i, j in PAIRS]
    share = [probs[p] for p in range(6)]
    mean = share[0] * pgrad[0]
    for p in range(1, 6):
        mean = mean + share[p] * pgrad[p]
    for p in range(6):
        lgrad = share[p] * (pgrad[p] - mean)
        first = beta_one * one[p] + (1.0 - beta_one) * lgrad
        second = beta_two * two[p] + (1.0 - beta_two) * lgrad * lgrad
        new_one[p] = first
        new_two[p] = second
        first_hat = first / (1.0 - beta_one**adam_step)
        second_hat = second / (1.0 - beta_two**adam_step)
        old = logits[p]
        new_logits[p] = old - rate * (first_hat / (jnp.sqrt(second_hat) + adam_eps) + decay * old)


def adam(wgrad, weight, probs, logits, one, two):
    cols = weight.shape[1]
    wide = WIDE
    three = pl.BlockSpec((6, 12, wide), lambda i: (0, 0, i))
    flat = pl.BlockSpec((ROWS, wide), lambda i: (0, i))
    out = jax.ShapeDtypeStruct((6, 12, cols), F32)
    return pl.pallas_call(
        adam_kernel,
        grid=(cols // wide,),
        in_specs=[flat, flat, three, three, three, three],
        out_specs=[three, three, three],
        out_shape=[out, out, out],
        scratch_shapes=[pltpu.VMEM((wide // 128 * ROWS, 128), F32)],
        compiler_params=pltpu.CompilerParams(vmem_limit_bytes=16 * MIB),
        cost_estimate=LIGHT,
    )(wgrad, weight, probs, logits, one, two)


def meet_kernel(place, mine, other, out):
    for i in range(64):
        at = pl.multiple_of(place[i] * ROWS, ROWS)
        out[pl.ds(at, ROWS), :128] = mine[i * ROWS : (i + 1) * ROWS, :]
        out[pl.ds(at, ROWS), 128:] = other[i * ROWS : (i + 1) * ROWS, :]


def meet(place, mine, other):
    return pl.pallas_call(
        meet_kernel,
        in_specs=[pl.BlockSpec(memory_space=pltpu.SMEM)] + [IN_VMEM] * 2,
        out_specs=IN_VMEM,
        out_shape=jax.ShapeDtypeStruct((3072, 256), BF16),
        compiler_params=pltpu.CompilerParams(vmem_limit_bytes=16 * MIB),
        cost_estimate=LIGHT,
    )(place, mine, other)


def part_kernel(place, *refs):
    mine, other = refs[-2:]
    at_block = 0
    for ref in refs[:-2]:
        for i in range(ref.shape[0] // ROWS):
            at = pl.multiple_of(place[at_block] * ROWS, ROWS)
            mine[pl.ds(at, ROWS), :] = ref[i * ROWS : (i + 1) * ROWS, :128]
            other[pl.ds(at, ROWS), :] = ref[i * ROWS : (i + 1) * ROWS, 128:]
            at_block += 1


def part(place, pieces):
    out = jax.ShapeDtypeStruct((3072, 128), F32)
    return pl.pallas_call(
        part_kernel,
        in_specs=[pl.BlockSpec(memory_space=pltpu.SMEM)] + [IN_VMEM] * len(pieces),
        out_specs=[IN_VMEM] * 2,
        out_shape=[out, out],
        compiler_params=pltpu.CompilerParams(vmem_limit_bytes=16 * MIB),
        cost_estimate=LIGHT,
    )(place, *pieces)


def share(acts, cot, start, count, at):
    return dot(acts[start : start + count, :], cot[:, at : at + TILE], ((1,), (0,)))


def line_kernel(*refs):
    out = refs[-1]
    for i, ref in enumerate(refs[:-1]):
        out[i * 96 : (i + 1) * 96, :] = ref[...]


def lead(acts, cot, start, base, up, down):
    for at in range(0, HALF, TILE):
        cols = slice(at, at + TILE)
        up[base : base + 192, cols] = share(acts, cot, start, 192, at).astype(BF16)
        down[base : base + 192, cols] = share(acts, cot, start + 192, 192, at).astype(BF16)


def follow(acts, cot, start_up, start_down, low, high, base, up, down):
    for at in range(0, HALF, TILE):
        cols = slice(at, at + TILE)
        got = share(acts, cot, start_up, 192, at) + low[base : base + 192, cols].astype(F32)
        up[:192, cols] = got.astype(BF16)
        up[192:384, cols] = share(acts, cot, start_up + 192, 192, at).astype(BF16)
        down[:192, cols] = share(acts, cot, start_down, 192, at).astype(BF16)
        got = share(acts, cot, start_down + 192, 192, at) + high[base : base + 192, cols].astype(F32)
        down[192:384, cols] = got.astype(BF16)


def second_kernel(start, acts, cot, near, far, up, down):
    up[:192, :] = far[192:384, :]
    down[:192, :] = near[:192, :]
    lead(acts, cot, start, 192, up, down)


def third_kernel(start_up, start_down, acts, cot, low, high, up, down):
    follow(acts, cot, start_up, start_down, low, high, 192, up, down)


def sum_kernel(own, one, two, three, out):
    total = own[...] + one[...].astype(F32) + two[...].astype(F32) + three[...].astype(F32)
    out[...] = total.astype(out.dtype)


def keep_kernel(start, acts, cot, up, down, own, *others):
    for at in range(0, HALF, TILE):
        cols = slice(at, at + TILE)
        for i in range(4):
            rows = slice(i * 96, i * 96 + 96)
            got = share(acts, cot, start + i * 96, 96, at)
            got = got + up[rows, cols].astype(F32) + down[rows, cols].astype(F32)
            if i == 0:
                own[:, cols] = got
            else:
                others[i - 1][:, cols] = got.astype(BF16)


def in_vmem(kernel, out_shape, *args, after=()):
    if after:
        inner, count, kept = kernel, len(args), len(args) + len(after)

        def kernel(*refs):
            inner(*refs[:count], *refs[kept:])

        args = args + tuple(after)
    return pl.pallas_call(
        kernel,
        in_specs=[IN_VMEM] * len(args),
        out_specs=[IN_VMEM] * len(out_shape),
        out_shape=out_shape,
        compiler_params=pltpu.CompilerParams(vmem_limit_bytes=24 * MIB),
        cost_estimate=LIGHT,
    )(*args)


def shape16(rows):
    return jax.ShapeDtypeStruct((rows, HALF), BF16)


def product_kernel(spans, first, acts, cot, *refs):
    size = len(spans)
    before = None if first else refs[0]
    refs = refs if first else refs[1:]
    pieces, result, grads = refs[:size], refs[size], refs[size + 1 :]
    for at in range(0, HALF, TILE):
        cols = slice(at, at + TILE)
        total = None if first else before[:, cols]
        for (start, skip, count), piece in zip(spans, pieces):
            rows = piece[skip : skip + count, cols]
            term = dot(acts[start : start + count, :], rows, ((0,), (0,)))
            total = term if total is None else total + term
        result[:, cols] = total
    for (start, skip, count), piece, grad in zip(spans, pieces, grads):
        grad[...] = dot(piece[skip : skip + count, :], cot[...], ((1,), (1,)))


def products(acts, cot, before, parts):
    first = before is None
    spans = [p[:3] for p in parts]
    shapes = [jax.ShapeDtypeStruct((256, HALF), F32)]
    shapes += [jax.ShapeDtypeStruct((p[2], 256), F32) for p in parts]
    args = [acts, cot] + ([] if first else [before]) + [p[3] for p in parts]
    return in_vmem(
        functools.partial(product_kernel, spans, first),
        shapes, *args
    )


def local(tokens, weight, logits, gumbel, cotangent, moment_one, moment_two):
    dp = lax.axis_index("dp")
    mp = lax.axis_index("mp")
    core, y, x, zh = dp % 2, (dp // 2) % 4, (dp // 8) % 4, dp // 32

    def half(value, which):
        return lax.dynamic_slice_in_dim(value, which * HALF, HALF, axis=1)

    whole = np.arange(64)
    dx, dy = (whole // 8 - x) % 4, (whole // 2 - y) % 4
    da, db = jnp.where(core == 0, dx, dy), jnp.where(core == 0, dy, dx)
    met_at = ((((whole // 32) ^ zh) * 4 + db) * 4 + da) * 2 + ((whole % 2) ^ core)
    met_at = met_at.astype(jnp.int32)
    order = np.arange(64)
    oz, ob, oa, oc = order // 32, (order // 8) % 4, (order // 2) % 4, order % 2
    ox, oy = jnp.where(core == 0, oa, ob), jnp.where(core == 0, ob, oa)
    lies_at = (((oz ^ zh) * 4 + (ox + x) % 4) * 4 + (oy + y) % 4) * 2 + (oc ^ core)
    lies_at = lies_at.astype(jnp.int32)

    probs, masked = make_masked(logits, gumbel, weight)
    block = jnp.concatenate([half(masked, core), send(half(masked, 1 - core), SIBLING)], axis=0)
    blocks = [block, send(block, PARTNER)]

    def start_of(dz, db):
        return (dz * 4 + db) * 384

    def spread_a(mine):
        return [mine, send(mine, A_DOWN), send(mine, A_TWO), send(mine, A_UP)]

    def kept(dz, up, down, after):
        own, one, two, three = in_vmem(
            functools.partial(keep_kernel, start_of(dz, 0)),
            [jax.ShapeDtypeStruct((96, HALF), F32)] + [shape16(96)] * 3, acts, cot, up, down,
            after=after,
        )
        return own, send(one, A_UP), send(two, A_TWO), send(three, A_DOWN)

    flipped = tokens.T
    own = jnp.concatenate([flipped, send(flipped, crossed(1))], axis=0)
    whole_x = jnp.concatenate([own, send(own, crossed(2))], axis=0)

    line0 = in_vmem(
        line_kernel, [shape16(384)], *spread_a(blocks[0]), after=(blocks[1], own)
    )[0]
    near0, far0 = send(line0, B_DOWN), send(line0, B_UP)
    line1 = in_vmem(line_kernel, [shape16(384)], *spread_a(blocks[1]), after=(whole_x,))[0]
    near1, far1 = send(line1, B_DOWN), send(line1, B_UP)

    came = jnp.concatenate([(mp ^ r) * 16 + np.arange(16) for r in range(4)])
    acts = meet(met_at[came], whole_x, send(whole_x, SIBLING))
    cot = jnp.concatenate(
        [half(cotangent, core), send(half(cotangent, 1 - core), SIBLING)], axis=0
    )

    up2, down2 = in_vmem(
        functools.partial(second_kernel, start_of(1, 2)),
        [shape16(384)] * 2, acts, cot, near0, far0, after=(line1,),
    )
    high0, low0 = send(up2, B_UP), send(down2, B_DOWN)
    up3, down3 = in_vmem(
        functools.partial(second_kernel, start_of(0, 2)),
        [shape16(384)] * 2, acts, cot, near1, far1, after=(up2,),
    )
    high1, low1 = send(up3, B_UP), send(down3, B_DOWN)
    up4, down4 = in_vmem(
        functools.partial(third_kernel, start_of(1, 1), start_of(1, 3)),
        [shape16(384)] * 2, acts, cot, high0, low0, after=(up3,),
    )
    up4, down4 = send(up4, B_UP), send(down4, B_DOWN)
    result, g0, g1, g3, g2, g4 = products(
        acts, cot, None,
        [
            (start_of(0, 0), 0, 384, line0),
            (start_of(0, 1), 0, 384, near0),
            (start_of(0, 3), 0, 384, far0),
            (start_of(0, 2), 0, 192, low0),
            (start_of(0, 2) + 192, 0, 192, high0),
        ],
    )
    up5, down5 = in_vmem(
        functools.partial(third_kernel, start_of(0, 1), start_of(0, 3)),
        [shape16(384)] * 2, acts, cot, high1, low1, after=(result,),
    )
    result, h0, h1, h3, h2, h4 = products(
        acts, cot, result,
        [
            (start_of(1, 0), 0, 384, line1),
            (start_of(1, 1), 0, 384, near1),
            (start_of(1, 3), 0, 384, far1),
            (start_of(1, 2), 0, 192, low1),
            (start_of(1, 2) + 192, 0, 192, high1),
        ],
    )
    up5, down5 = send(up5, B_UP), send(down5, B_DOWN)
    mine, theirs = part(lies_at, [g0, g1, g2, g4, g3, h0, h1, h2, h4, h3])
    grad = mine + send(theirs, SIBLING)
    total = lax.psum_scatter(grad, "mp", scatter_dimension=0, tiled=True)

    sums = in_vmem(sum_kernel, [shape16(96)], *kept(1, up4, down4, (mine,)), after=(grad,))
    sums += in_vmem(
        sum_kernel,
        [jax.ShapeDtypeStruct((96, HALF), F32)], *kept(0, up5, down5, (sums[0],)),
    )
    wsum = sums[1] + send(sums[0], PARTNER).astype(F32)
    other = send(wsum[ROWS:], SIBLING)
    wgrad = jnp.where(
        core == 0,
        jnp.concatenate([wsum[:ROWS], other], axis=1),
        jnp.concatenate([other, wsum[:ROWS]], axis=1),
    )
    new_logits, new_one, new_two = adam(wgrad, weight, probs, logits, moment_one, moment_two)

    result = result.astype(BF16)
    other = send(result[128:], SIBLING)
    output = jnp.where(
        core == 0,
        jnp.concatenate([result[:128], other], axis=1),
        jnp.concatenate([other, result[:128]], axis=1),
    )

    input_grad = total.astype(BF16).T
    return (output, input_grad, new_logits, new_one, new_two)


def solution(mesh):
    placed = (
        P("dp", "mp"),
        P("dp", "mp"),
        P(None, "dp", "mp"),
        P(None, "dp", "mp"),
        P("dp", "mp"),
        P(None, "dp", "mp"),
        P(None, "dp", "mp"),
    )
    return jax.shard_map(
        local,
        mesh=mesh,
        in_specs=placed,
        out_specs=(
            P("dp", "mp"),
            P("dp", "mp"),
            P(None, "dp", "mp"),
            P(None, "dp", "mp"),
            P(None, "dp", "mp"),
        ),
        check_vma=False,
    )
```

```python
import functools

import jax
import jax.numpy as jnp
import numpy as np
from jax import lax
from jax.experimental import pallas as pl
from jax.experimental.pallas import tpu as pltpu
from jax.sharding import PartitionSpec as P

beta_one = 0.9
beta_two = 0.999
adam_eps = 1e-08
decay = 0.01
rate = 0.1
adam_step = 10.0

F32 = jnp.float32
BF16 = jnp.bfloat16
AXES = ("dp", "mp")
SIZES = (2, 4, 4, 2, 4)
PAIRS = tuple((i, j) for i in range(4) for j in range(i + 1, 4))
ROWS = 48
HALF = 1536
WIDE = 512
TILE = 512
MIB = 1 << 20
IN_VMEM = pl.BlockSpec(memory_space=pltpu.VMEM)
HEAVY = pl.CostEstimate(flops=20000000000, bytes_accessed=1, transcendentals=0)
LIGHT = pl.CostEstimate(flops=0, bytes_accessed=1, transcendentals=0)


def pairs_of(target):
    found = []
    for here in np.ndindex(*SIZES):
        there = tuple(a % b for a, b in zip(target(*here), SIZES))
        found.append(
            (int(np.ravel_multi_index(here, SIZES)), int(np.ravel_multi_index(there, SIZES)))
        )
    return found


def step_a(by):
    return pairs_of(
        lambda z, x, y, c, m: (z, x + by, y, c, m) if c == 0 else (z, x, y + by, c, m)
    )


def step_b(by):
    return pairs_of(
        lambda z, x, y, c, m: (z, x, y + by, c, m) if c == 0 else (z, x + by, y, c, m)
    )


SIBLING = pairs_of(lambda z, x, y, c, m: (z, x, y, c + 1, m))
PARTNER = pairs_of(lambda z, x, y, c, m: (z + 1, x, y, c, m))
A_UP, A_DOWN, A_TWO = step_a(1), step_a(-1), step_a(2)
B_UP, B_DOWN = step_b(1), step_b(-1)


def around(by):
    return pairs_of(lambda z, x, y, c, m: (z, x, y, c, m + by))


def crossed(by):
    return pairs_of(lambda z, x, y, c, m: (z, x, y, c, m ^ by))


def send(value, pairs):
    return lax.ppermute(value, AXES, pairs)


def dot(a, b, dims):
    return lax.dot_general(a, b, (dims, ((), ())), preferred_element_type=F32)


def mask_kernel(logits, gumbel, weight, probs, masked, spread):
    scores = [logits[p] + gumbel[p].astype(F32) for p in range(6)]
    top = scores[0]
    for p in range(1, 6):
        top = jnp.maximum(top, scores[p])
    exps = [jnp.exp(s - top) for s in scores]
    total = exps[0]
    for p in range(1, 6):
        total = total + exps[p]
    share = [e / total for e in exps]
    for p in range(6):
        probs[p] = share[p]
    for slot in range(4):
        kept = [share[p] for p in range(6) if slot in PAIRS[p]]
        mask = kept[0] + kept[1] + kept[2]
        for j in range(WIDE // 128):
            at = j * 128
            spread[pl.ds(j * ROWS + slot, 12, stride=4), :] = mask[:, at : at + 128]
    for j in range(WIDE // 128):
        at = j * 128
        part = weight[:, at : at + 128].astype(F32) * spread[j * ROWS : (j + 1) * ROWS, :]
        masked[:, at : at + 128] = part.astype(BF16)


def make_masked(logits, gumbel, weight):
    cols = weight.shape[1]
    wide = WIDE
    three = pl.BlockSpec((6, 12, wide), lambda i: (0, 0, i))
    two = pl.BlockSpec((ROWS, wide), lambda i: (0, i))
    return pl.pallas_call(
        mask_kernel,
        grid=(cols // wide,),
        in_specs=[three, three, two],
        out_specs=[three, two],
        out_shape=[
            jax.ShapeDtypeStruct((6, 12, cols), F32),
            jax.ShapeDtypeStruct((ROWS, cols), BF16),
        ],
        scratch_shapes=[pltpu.VMEM((wide // 128 * ROWS, 128), F32)],
        compiler_params=pltpu.CompilerParams(vmem_limit_bytes=16 * MIB),
        cost_estimate=LIGHT,
    )(logits, gumbel, weight)


def adam_kernel(wgrad, weight, probs, logits, one, two, new_logits, new_one, new_two, spread):
    for j in range(WIDE // 128):
        at = j * 128
        spread[j * ROWS : (j + 1) * ROWS, :] = (
            weight[:, at : at + 128].astype(F32) * wgrad[:, at : at + 128]
        )
    slots = [
        jnp.concatenate(
            [spread[pl.ds(j * ROWS + slot, 12, stride=4), :] for j in range(WIDE // 128)], axis=1
        )
        for slot in range(4)
    ]
    pgrad = [slots[i] + slots[j] for i, j in PAIRS]
    share = [probs[p] for p in range(6)]
    mean = share[0] * pgrad[0]
    for p in range(1, 6):
        mean = mean + share[p] * pgrad[p]
    for p in range(6):
        lgrad = share[p] * (pgrad[p] - mean)
        first = beta_one * one[p] + (1.0 - beta_one) * lgrad
        second = beta_two * two[p] + (1.0 - beta_two) * lgrad * lgrad
        new_one[p] = first
        new_two[p] = second
        first_hat = first / (1.0 - beta_one**adam_step)
        second_hat = second / (1.0 - beta_two**adam_step)
        old = logits[p]
        new_logits[p] = old - rate * (first_hat / (jnp.sqrt(second_hat) + adam_eps) + decay * old)


def adam(wgrad, weight, probs, logits, one, two):
    cols = weight.shape[1]
    wide = WIDE
    three = pl.BlockSpec((6, 12, wide), lambda i: (0, 0, i))
    flat = pl.BlockSpec((ROWS, wide), lambda i: (0, i))
    out = jax.ShapeDtypeStruct((6, 12, cols), F32)
    return pl.pallas_call(
        adam_kernel,
        grid=(cols // wide,),
        in_specs=[flat, flat, three, three, three, three],
        out_specs=[three, three, three],
        out_shape=[out, out, out],
        scratch_shapes=[pltpu.VMEM((wide // 128 * ROWS, 128), F32)],
        compiler_params=pltpu.CompilerParams(vmem_limit_bytes=16 * MIB),
        cost_estimate=LIGHT,
    )(wgrad, weight, probs, logits, one, two)


def meet_kernel(place, mine, other, out):
    for i in range(64):
        at = pl.multiple_of(place[i] * ROWS, ROWS)
        out[pl.ds(at, ROWS), :128] = mine[i * ROWS : (i + 1) * ROWS, :]
        out[pl.ds(at, ROWS), 128:] = other[i * ROWS : (i + 1) * ROWS, :]


def meet(place, mine, other):
    return pl.pallas_call(
        meet_kernel,
        in_specs=[pl.BlockSpec(memory_space=pltpu.SMEM)] + [IN_VMEM] * 2,
        out_specs=IN_VMEM,
        out_shape=jax.ShapeDtypeStruct((3072, 256), BF16),
        compiler_params=pltpu.CompilerParams(vmem_limit_bytes=16 * MIB),
        cost_estimate=LIGHT,
    )(place, mine, other)


BLOCKS = (
    (*range(0, 16), *range(24, 32)),
    tuple(range(16, 24)),
    (*range(32, 48), *range(56, 64)),
    tuple(range(48, 56)),
)


def fold_kernel(place, *refs):
    keep, give, total = refs[-3:]
    for group, blocks in enumerate(BLOCKS):
        for i, block in enumerate(blocks):
            at = pl.multiple_of(place[block] * ROWS, ROWS)
            total[pl.ds(at, ROWS), :] = refs[group][i * ROWS : (i + 1) * ROWS, :]
    for group, blocks in enumerate(BLOCKS):
        for i, block in enumerate(blocks):
            at = pl.multiple_of(place[64 + block] * ROWS, ROWS)
            rows = pl.ds(at, ROWS)
            total[rows, :] = total[rows, :] + refs[4 + group][i * ROWS : (i + 1) * ROWS, :]
    keep[...] = total[:1536, :]
    give[...] = total[1536:, :]


def half_kernel(place, mine, other, keep, give):
    at = pl.multiple_of(place[0] * 768, 768)
    keep[...] = mine[pl.ds(at, 768), :] + other[pl.ds(at, 768), :]
    at = pl.multiple_of((1 - place[0]) * 768, 768)
    give[...] = mine[pl.ds(at, 768), :] + other[pl.ds(at, 768), :]


def fold(kernel, place, rows, *parts, scratch=()):
    out = jax.ShapeDtypeStruct((rows, 128), F32)
    return pl.pallas_call(
        kernel,
        in_specs=[pl.BlockSpec(memory_space=pltpu.SMEM)] + [IN_VMEM] * len(parts),
        out_specs=[IN_VMEM] * 2,
        out_shape=[out, out],
        scratch_shapes=scratch,
        compiler_params=pltpu.CompilerParams(vmem_limit_bytes=16 * MIB),
        cost_estimate=LIGHT,
    )(place.astype(jnp.int32), *parts)


def share(acts, cot, start, count, at):
    return dot(acts[start : start + count, :], cot[:, at : at + TILE], ((1,), (0,)))


def stack_kernel(*refs):
    out, at = refs[-1], 0
    for ref in refs[:-1]:
        out[at : at + ref.shape[0], :] = ref[...]
        at += ref.shape[0]


def lead(acts, cot, start, base, up, down):
    for at in range(0, HALF, TILE):
        cols = slice(at, at + TILE)
        up[base : base + 192, cols] = share(acts, cot, start, 192, at).astype(BF16)
        down[base : base + 192, cols] = share(acts, cot, start + 192, 192, at).astype(BF16)


def follow(acts, cot, start_up, start_down, low, high, base, up, down):
    for at in range(0, HALF, TILE):
        cols = slice(at, at + TILE)
        got = share(acts, cot, start_up, 192, at) + low[base : base + 192, cols].astype(F32)
        up[:192, cols] = got.astype(BF16)
        up[192:384, cols] = share(acts, cot, start_up + 192, 192, at).astype(BF16)
        down[:192, cols] = share(acts, cot, start_down, 192, at).astype(BF16)
        got = share(acts, cot, start_down + 192, 192, at) + high[base : base + 192, cols].astype(F32)
        down[192:384, cols] = got.astype(BF16)


def second_kernel(start, acts, cot, near, far, up, down):
    up[:192, :] = far[192:384, :]
    down[:192, :] = near[:192, :]
    lead(acts, cot, start, 192, up, down)


def third_kernel(start_up, start_down, acts, cot, low, high, up, down):
    follow(acts, cot, start_up, start_down, low, high, 192, up, down)


def sum_kernel(own, one, two, three, out):
    total = own[...] + one[...].astype(F32) + two[...].astype(F32) + three[...].astype(F32)
    out[...] = total.astype(out.dtype)


def keep_kernel(start, acts, cot, up, down, own, *others):
    for at in range(0, HALF, TILE):
        cols = slice(at, at + TILE)
        for i in range(4):
            rows = slice(i * 96, i * 96 + 96)
            got = share(acts, cot, start + i * 96, 96, at)
            got = got + up[rows, cols].astype(F32) + down[rows, cols].astype(F32)
            if i == 0:
                own[:, cols] = got
            else:
                others[i - 1][:, cols] = got.astype(BF16)


def in_vmem(kernel, out_shape, *args, after=(), cost=LIGHT):
    if after:
        inner, count, kept = kernel, len(args), len(args) + len(after)

        def kernel(*refs):
            inner(*refs[:count], *refs[kept:])

        args = args + tuple(after)
    return pl.pallas_call(
        kernel,
        in_specs=[IN_VMEM] * len(args),
        out_specs=[IN_VMEM] * len(out_shape),
        out_shape=out_shape,
        compiler_params=pltpu.CompilerParams(vmem_limit_bytes=24 * MIB),
        cost_estimate=cost,
    )(*args)


def shape16(rows):
    return jax.ShapeDtypeStruct((rows, HALF), BF16)


def product_kernel(spans, first, acts, cot, *refs):
    size = len(spans)
    before = None if first else refs[0]
    refs = refs if first else refs[1:]
    pieces, (result, mine, theirs) = refs[:size], refs[size:]
    for at in range(0, HALF, TILE):
        cols = slice(at, at + TILE)
        total = None if first else before[:, cols]
        for (start, skip, count), piece in zip(spans, pieces):
            rows = piece[skip : skip + count, cols]
            term = dot(acts[start : start + count, :], rows, ((0,), (0,)))
            total = term if total is None else total + term
        result[:, cols] = total
    at = 0
    for (start, skip, count), piece in zip(spans, pieces):
        grad = dot(piece[skip : skip + count, :], cot[...], ((1,), (1,)))
        mine[at : at + count, :] = grad[:, :128]
        theirs[at : at + count, :] = grad[:, 128:]
        at += count


def products(acts, cot, before, parts, after, cost=HEAVY):
    first = before is None
    spans = [p[:3] for p in parts]
    columns = jax.ShapeDtypeStruct((sum(p[2] for p in parts), 128), F32)
    shapes = [jax.ShapeDtypeStruct((256, HALF), F32), columns, columns]
    args = [acts, cot] + ([] if first else [before]) + [p[3] for p in parts]
    result, mine, theirs = in_vmem(
        functools.partial(product_kernel, spans, first), shapes, *args, after=after, cost=cost
    )
    return result, mine, send(theirs, SIBLING)


def local(tokens, weight, logits, gumbel, cotangent, moment_one, moment_two):
    dp = lax.axis_index("dp")
    mp = lax.axis_index("mp")
    core, y, x, zh = dp % 2, (dp // 2) % 4, (dp // 8) % 4, dp // 32

    def half(value, which):
        return lax.dynamic_slice_in_dim(value, which * HALF, HALF, axis=1)

    whole = np.arange(64)
    dx, dy = (whole // 8 - x) % 4, (whole // 2 - y) % 4
    da, db = jnp.where(core == 0, dx, dy), jnp.where(core == 0, dy, dx)
    met_at = ((((whole // 32) ^ zh) * 4 + db) * 4 + da) * 2 + ((whole % 2) ^ core)
    met_at = met_at.astype(jnp.int32)
    order = np.arange(64)
    oz, ob, oa, oc = order // 32, (order // 8) % 4, (order // 2) % 4, order % 2

    def folded_at(side):
        ox, oy = jnp.where(side == 0, oa, ob), jnp.where(side == 0, ob, oa)
        block = (((oz ^ zh) * 4 + (ox + x) % 4) * 4 + (oy + y) % 4) * 2 + (oc ^ side)
        quarter = block // 16
        return ((((quarter % 2) ^ (mp % 2)) * 2 + quarter // 2) * 16) + block % 16


    flipped = tokens.T
    crossed_x = send(flipped, crossed(1))
    probs, masked = make_masked(logits, gumbel, weight)
    block = in_vmem(
        stack_kernel, [shape16(96)],
        half(masked, core), send(half(masked, 1 - core), SIBLING), after=(crossed_x,),
    )[0]
    blocks = [block, send(block, PARTNER)]

    def start_of(dz, db):
        return (dz * 4 + db) * 384

    def spread_a(mine):
        return [mine, send(mine, A_DOWN), send(mine, A_TWO), send(mine, A_UP)]

    def kept(dz, up, down, after):
        own, one, two, three = in_vmem(
            functools.partial(keep_kernel, start_of(dz, 0)),
            [jax.ShapeDtypeStruct((96, HALF), F32)] + [shape16(96)] * 3, acts, cot, up, down,
            after=after,
        )
        return own, send(one, A_UP), send(two, A_TWO), send(three, A_DOWN)

    cot = jnp.concatenate(
        [half(cotangent, core), send(half(cotangent, 1 - core), SIBLING)], axis=0
    )
    line0 = in_vmem(
        stack_kernel, [shape16(384)], *spread_a(blocks[0]), after=(blocks[1], cot)
    )[0]
    near0, far0 = send(line0, B_DOWN), send(line0, B_UP)
    own = in_vmem(
        stack_kernel, [jax.ShapeDtypeStruct((1536, 128), BF16)], flipped, crossed_x, after=(line0,)
    )[0]
    line1 = in_vmem(stack_kernel, [shape16(384)], *spread_a(blocks[1]))[0]
    near1, far1 = send(line1, B_DOWN), send(line1, B_UP)
    whole_x = in_vmem(
        stack_kernel, [jax.ShapeDtypeStruct((3072, 128), BF16)],
        own, send(own, crossed(2)), after=(line1,),
    )[0]

    came = jnp.concatenate([(mp ^ r) * 16 + np.arange(16) for r in range(4)])
    acts = meet(met_at[came], whole_x, send(whole_x, SIBLING))
    up2, down2 = in_vmem(
        functools.partial(second_kernel, start_of(1, 2)),
        [shape16(384)] * 2, acts, cot, near0, far0, after=(line1,),
    )
    high0, low0 = send(up2, B_UP), send(down2, B_DOWN)
    result, *grad_a = products(
        acts, cot, None,
        [
            (start_of(0, 0), 0, 384, line0),
            (start_of(0, 1), 0, 384, near0),
            (start_of(0, 3), 0, 384, far0),
        ],
        (up2,),
    )
    up3, down3 = in_vmem(
        functools.partial(second_kernel, start_of(0, 2)),
        [shape16(384)] * 2, acts, cot, near1, far1, after=(result,),
    )
    result, *grad_c = products(
        acts, cot, result,
        [
            (start_of(1, 0), 0, 384, line1),
            (start_of(1, 1), 0, 384, near1),
            (start_of(1, 3), 0, 384, far1),
        ],
        (up3,),
    )
    high1, low1 = send(up3, B_UP), send(down3, B_DOWN)
    up4, down4 = in_vmem(
        functools.partial(third_kernel, start_of(1, 1), start_of(1, 3)),
        [shape16(384)] * 2, acts, cot, high0, low0, after=(result,),
    )
    result, *grad_b = products(
        acts, cot, result,
        [(start_of(0, 2), 0, 192, low0), (start_of(0, 2) + 192, 0, 192, high0)],
        (up4,), LIGHT,
    )
    up4, down4 = send(up4, B_UP), send(down4, B_DOWN)
    up5, down5 = in_vmem(
        functools.partial(third_kernel, start_of(0, 1), start_of(0, 3)),
        [shape16(384)] * 2, acts, cot, high1, low1,
        after=(grad_a[1], grad_b[1], grad_c[1]),
    )
    result, *grad_d = products(
        acts, cot, result,
        [(start_of(1, 2), 0, 192, low1), (start_of(1, 2) + 192, 0, 192, high1)],
        (up4,), LIGHT,
    )
    up5, down5 = send(up5, B_UP), send(down5, B_DOWN)
    both = zip(grad_a, grad_b, grad_c, grad_d)
    keep, give = fold(
        fold_kernel, jnp.concatenate([folded_at(core), folded_at(1 - core)]), 1536,
        *next(both), *next(both), scratch=[pltpu.VMEM((3072, 128), F32)],
    )
    own_part, give = fold(
        half_kernel, jnp.reshape(mp // 2, (1,)), 768, keep, send(give, crossed(1))
    )
    total = own_part + send(give, crossed(2))

    sums = in_vmem(sum_kernel, [shape16(96)], *kept(1, up4, down4, ()))
    sums += in_vmem(
        sum_kernel,
        [jax.ShapeDtypeStruct((96, HALF), F32)], *kept(0, up5, down5, (sums[0],)),
        after=(own_part,),
    )
    wsum = sums[1] + send(sums[0], PARTNER).astype(F32)
    other = send(wsum[ROWS:], SIBLING)
    wgrad = jnp.where(
        core == 0,
        jnp.concatenate([wsum[:ROWS], other], axis=1),
        jnp.concatenate([other, wsum[:ROWS]], axis=1),
    )
    new_logits, new_one, new_two = adam(wgrad, weight, probs, logits, moment_one, moment_two)

    result = result.astype(BF16)
    other = send(result[128:], SIBLING)
    output = jnp.where(
        core == 0,
        jnp.concatenate([result[:128], other], axis=1),
        jnp.concatenate([other, result[:128]], axis=1),
    )

    input_grad = total.astype(BF16).T
    return (output, input_grad, new_logits, new_one, new_two)


def solution(mesh):
    placed = (
        P("dp", "mp"),
        P("dp", "mp"),
        P(None, "dp", "mp"),
        P(None, "dp", "mp"),
        P("dp", "mp"),
        P(None, "dp", "mp"),
        P(None, "dp", "mp"),
    )
    return jax.shard_map(
        local,
        mesh=mesh,
        in_specs=placed,
        out_specs=(
            P("dp", "mp"),
            P("dp", "mp"),
            P(None, "dp", "mp"),
            P(None, "dp", "mp"),
            P(None, "dp", "mp"),
        ),
        check_vma=False,
    )
```

```python
import functools

import jax
import jax.numpy as jnp
import numpy as np
from jax import lax
from jax.experimental import pallas as pl
from jax.experimental.pallas import tpu as pltpu
from jax.sharding import PartitionSpec as P

beta_one = 0.9
beta_two = 0.999
adam_eps = 1e-08
decay = 0.01
rate = 0.1
adam_step = 10.0

F32 = jnp.float32
BF16 = jnp.bfloat16
AXES = ("dp", "mp")
SIZES = (2, 4, 4, 2, 4)
PAIRS = tuple((i, j) for i in range(4) for j in range(i + 1, 4))
ROWS = 48
HALF = 1536
WIDE = 512
TILE = 512
MIB = 1 << 20
IN_VMEM = pl.BlockSpec(memory_space=pltpu.VMEM)
HEAVY = pl.CostEstimate(flops=20000000000, bytes_accessed=1, transcendentals=0)
LIGHT = pl.CostEstimate(flops=0, bytes_accessed=1, transcendentals=0)


def pairs_of(target):
    found = []
    for here in np.ndindex(*SIZES):
        there = tuple(a % b for a, b in zip(target(*here), SIZES))
        found.append(
            (int(np.ravel_multi_index(here, SIZES)), int(np.ravel_multi_index(there, SIZES)))
        )
    return found


def step_a(by):
    return pairs_of(
        lambda z, x, y, c, m: (z, x + by, y, c, m) if c == 0 else (z, x, y + by, c, m)
    )


def step_b(by):
    return pairs_of(
        lambda z, x, y, c, m: (z, x, y + by, c, m) if c == 0 else (z, x + by, y, c, m)
    )


SIBLING = pairs_of(lambda z, x, y, c, m: (z, x, y, c + 1, m))
PARTNER = pairs_of(lambda z, x, y, c, m: (z + 1, x, y, c, m))
A_UP, A_DOWN, A_TWO = step_a(1), step_a(-1), step_a(2)
B_UP, B_DOWN = step_b(1), step_b(-1)


def around(by):
    return pairs_of(lambda z, x, y, c, m: (z, x, y, c, m + by))


def crossed(by):
    return pairs_of(lambda z, x, y, c, m: (z, x, y, c, m ^ by))


def send(value, pairs):
    return lax.ppermute(value, AXES, pairs)


def dot(a, b, dims):
    return lax.dot_general(a, b, (dims, ((), ())), preferred_element_type=F32)


def mask_kernel(logits, gumbel, weight, probs, masked, spread):
    scores = [logits[p] + gumbel[p].astype(F32) for p in range(6)]
    top = scores[0]
    for p in range(1, 6):
        top = jnp.maximum(top, scores[p])
    exps = [jnp.exp(s - top) for s in scores]
    total = exps[0]
    for p in range(1, 6):
        total = total + exps[p]
    share = [e / total for e in exps]
    for p in range(6):
        probs[p] = share[p]
    for slot in range(4):
        kept = [share[p] for p in range(6) if slot in PAIRS[p]]
        mask = kept[0] + kept[1] + kept[2]
        for j in range(WIDE // 128):
            at = j * 128
            spread[pl.ds(j * ROWS + slot, 12, stride=4), :] = mask[:, at : at + 128]
    for j in range(WIDE // 128):
        at = j * 128
        part = weight[:, at : at + 128].astype(F32) * spread[j * ROWS : (j + 1) * ROWS, :]
        masked[:, at : at + 128] = part.astype(BF16)


def make_masked(logits, gumbel, weight):
    cols = weight.shape[1]
    wide = WIDE
    three = pl.BlockSpec((6, 12, wide), lambda i: (0, 0, i))
    two = pl.BlockSpec((ROWS, wide), lambda i: (0, i))
    return pl.pallas_call(
        mask_kernel,
        grid=(cols // wide,),
        in_specs=[three, three, two],
        out_specs=[three, two],
        out_shape=[
            jax.ShapeDtypeStruct((6, 12, cols), F32),
            jax.ShapeDtypeStruct((ROWS, cols), BF16),
        ],
        scratch_shapes=[pltpu.VMEM((wide // 128 * ROWS, 128), F32)],
        compiler_params=pltpu.CompilerParams(vmem_limit_bytes=16 * MIB),
        cost_estimate=LIGHT,
    )(logits, gumbel, weight)


def adam_kernel(wgrad, weight, probs, logits, one, two, new_logits, new_one, new_two, spread):
    for j in range(WIDE // 128):
        at = j * 128
        spread[j * ROWS : (j + 1) * ROWS, :] = (
            weight[:, at : at + 128].astype(F32) * wgrad[:, at : at + 128]
        )
    slots = [
        jnp.concatenate(
            [spread[pl.ds(j * ROWS + slot, 12, stride=4), :] for j in range(WIDE // 128)], axis=1
        )
        for slot in range(4)
    ]
    pgrad = [slots[i] + slots[j] for i, j in PAIRS]
    share = [probs[p] for p in range(6)]
    mean = share[0] * pgrad[0]
    for p in range(1, 6):
        mean = mean + share[p] * pgrad[p]
    for p in range(6):
        lgrad = share[p] * (pgrad[p] - mean)
        first = beta_one * one[p] + (1.0 - beta_one) * lgrad
        second = beta_two * two[p] + (1.0 - beta_two) * lgrad * lgrad
        new_one[p] = first
        new_two[p] = second
        first_hat = first / (1.0 - beta_one**adam_step)
        second_hat = second / (1.0 - beta_two**adam_step)
        old = logits[p]
        new_logits[p] = old - rate * (first_hat / (jnp.sqrt(second_hat) + adam_eps) + decay * old)


def adam(wgrad, weight, probs, logits, one, two):
    cols = weight.shape[1]
    wide = WIDE
    three = pl.BlockSpec((6, 12, wide), lambda i: (0, 0, i))
    flat = pl.BlockSpec((ROWS, wide), lambda i: (0, i))
    out = jax.ShapeDtypeStruct((6, 12, cols), F32)
    return pl.pallas_call(
        adam_kernel,
        grid=(cols // wide,),
        in_specs=[flat, flat, three, three, three, three],
        out_specs=[three, three, three],
        out_shape=[out, out, out],
        scratch_shapes=[pltpu.VMEM((wide // 128 * ROWS, 128), F32)],
        compiler_params=pltpu.CompilerParams(vmem_limit_bytes=16 * MIB),
        cost_estimate=LIGHT,
    )(wgrad, weight, probs, logits, one, two)


def meet_kernel(place, mine, other, out):
    for i in range(64):
        at = pl.multiple_of(place[i] * ROWS, ROWS)
        out[pl.ds(at, ROWS), :128] = mine[i * ROWS : (i + 1) * ROWS, :]
        out[pl.ds(at, ROWS), 128:] = other[i * ROWS : (i + 1) * ROWS, :]


def meet(place, mine, other):
    return pl.pallas_call(
        meet_kernel,
        in_specs=[pl.BlockSpec(memory_space=pltpu.SMEM)] + [IN_VMEM] * 2,
        out_specs=IN_VMEM,
        out_shape=jax.ShapeDtypeStruct((3072, 256), BF16),
        compiler_params=pltpu.CompilerParams(vmem_limit_bytes=16 * MIB),
        cost_estimate=LIGHT,
    )(place, mine, other)


BLOCKS = (
    (*range(0, 16), *range(24, 32), *range(16, 24)),
    (*range(32, 48), *range(56, 64), *range(48, 56)),
)


def fold_kernel(place, *refs):
    keep, give, total = refs[-3:]
    for group, blocks in enumerate(BLOCKS):
        for i, block in enumerate(blocks):
            at = pl.multiple_of(place[block] * ROWS, ROWS)
            total[pl.ds(at, ROWS), :] = refs[group][i * ROWS : (i + 1) * ROWS, :]
    for group, blocks in enumerate(BLOCKS):
        for i, block in enumerate(blocks):
            at = pl.multiple_of(place[64 + block] * ROWS, ROWS)
            rows = pl.ds(at, ROWS)
            total[rows, :] = total[rows, :] + refs[2 + group][i * ROWS : (i + 1) * ROWS, :]
    keep[...] = total[:1536, :]
    give[...] = total[1536:, :]


def half_kernel(place, mine, other, keep, give):
    at = pl.multiple_of(place[0] * 768, 768)
    keep[...] = mine[pl.ds(at, 768), :] + other[pl.ds(at, 768), :]
    at = pl.multiple_of((1 - place[0]) * 768, 768)
    give[...] = mine[pl.ds(at, 768), :] + other[pl.ds(at, 768), :]


def fold(kernel, place, rows, *parts, scratch=()):
    out = jax.ShapeDtypeStruct((rows, 128), F32)
    return pl.pallas_call(
        kernel,
        in_specs=[pl.BlockSpec(memory_space=pltpu.SMEM)] + [IN_VMEM] * len(parts),
        out_specs=[IN_VMEM] * 2,
        out_shape=[out, out],
        scratch_shapes=scratch,
        compiler_params=pltpu.CompilerParams(vmem_limit_bytes=16 * MIB),
        cost_estimate=LIGHT,
    )(place.astype(jnp.int32), *parts)


def share(acts, cot, start, count, at):
    return dot(acts[start : start + count, :], cot[:, at : at + TILE], ((1,), (0,)))


def stack_kernel(*refs):
    out, at = refs[-1], 0
    for ref in refs[:-1]:
        out[at : at + ref.shape[0], :] = ref[...]
        at += ref.shape[0]


def lead(acts, cot, start, base, up, down):
    for at in range(0, HALF, TILE):
        cols = slice(at, at + TILE)
        up[base : base + 192, cols] = share(acts, cot, start, 192, at).astype(BF16)
        down[base : base + 192, cols] = share(acts, cot, start + 192, 192, at).astype(BF16)


def follow(acts, cot, start_up, start_down, low, high, base, up, down):
    for at in range(0, HALF, TILE):
        cols = slice(at, at + TILE)
        got = share(acts, cot, start_up, 192, at) + low[base : base + 192, cols].astype(F32)
        up[:192, cols] = got.astype(BF16)
        up[192:384, cols] = share(acts, cot, start_up + 192, 192, at).astype(BF16)
        down[:192, cols] = share(acts, cot, start_down, 192, at).astype(BF16)
        got = share(acts, cot, start_down + 192, 192, at) + high[base : base + 192, cols].astype(F32)
        down[192:384, cols] = got.astype(BF16)


def second_kernel(start, acts, cot, near, far, up, down):
    up[:192, :] = far[192:384, :]
    down[:192, :] = near[:192, :]
    lead(acts, cot, start, 192, up, down)


def third_kernel(start_up, start_down, acts, cot, low, high, up, down):
    follow(acts, cot, start_up, start_down, low, high, 192, up, down)


def sum_kernel(own, one, two, three, out):
    total = own[...] + one[...].astype(F32) + two[...].astype(F32) + three[...].astype(F32)
    out[...] = total.astype(out.dtype)


def keep_kernel(start, acts, cot, up, down, own, *others):
    for at in range(0, HALF, TILE):
        cols = slice(at, at + TILE)
        for i in range(4):
            rows = slice(i * 96, i * 96 + 96)
            got = share(acts, cot, start + i * 96, 96, at)
            got = got + up[rows, cols].astype(F32) + down[rows, cols].astype(F32)
            if i == 0:
                own[:, cols] = got
            else:
                others[i - 1][:, cols] = got.astype(BF16)


def in_vmem(kernel, out_shape, *args, after=(), cost=LIGHT):
    if after:
        inner, count, kept = kernel, len(args), len(args) + len(after)

        def kernel(*refs):
            inner(*refs[:count], *refs[kept:])

        args = args + tuple(after)
    return pl.pallas_call(
        kernel,
        in_specs=[IN_VMEM] * len(args),
        out_specs=[IN_VMEM] * len(out_shape),
        out_shape=out_shape,
        compiler_params=pltpu.CompilerParams(vmem_limit_bytes=24 * MIB),
        cost_estimate=cost,
    )(*args)


def shape16(rows):
    return jax.ShapeDtypeStruct((rows, HALF), BF16)


def product_kernel(spans, first, joined, acts, cot, *refs):
    size = len(spans)
    before = None if first else refs[0]
    refs = refs if first else refs[1:]
    pieces, (result, mine, theirs) = refs[:size], refs[-3:]
    for at in range(0, HALF, TILE):
        cols = slice(at, at + TILE)
        total = None if first else before[:, cols]
        for (start, skip, count), piece in zip(spans, pieces):
            rows = piece[skip : skip + count, cols]
            term = dot(acts[start : start + count, :], rows, ((0,), (0,)))
            total = term if total is None else total + term
        result[:, cols] = total.astype(result.dtype)
    at = 0
    if joined:
        at = refs[size].shape[0]
        mine[:at, :] = refs[size][...]
        theirs[:at, :] = refs[size + 1][...]
    for (start, skip, count), piece in zip(spans, pieces):
        grad = dot(piece[skip : skip + count, :], cot[...], ((1,), (1,)))
        mine[at : at + count, :] = grad[:, :128]
        theirs[at : at + count, :] = grad[:, 128:]
        at += count


def products(acts, cot, before, parts, after, cost=HEAVY, kind=F32, joined=()):
    first = before is None
    spans = [p[:3] for p in parts]
    rows = sum(p[2] for p in parts) + (joined[0].shape[0] if joined else 0)
    columns = jax.ShapeDtypeStruct((rows, 128), F32)
    shapes = [jax.ShapeDtypeStruct((256, HALF), kind), columns, columns]
    args = [acts, cot] + ([] if first else [before]) + [p[3] for p in parts] + list(joined)
    kernel = functools.partial(product_kernel, spans, first, bool(joined))
    return in_vmem(kernel, shapes, *args, after=after, cost=cost)


def local(tokens, weight, logits, gumbel, cotangent, moment_one, moment_two):
    dp = lax.axis_index("dp")
    mp = lax.axis_index("mp")
    core, y, x, zh = dp % 2, (dp // 2) % 4, (dp // 8) % 4, dp // 32

    def half(value, which):
        return lax.dynamic_slice_in_dim(value, which * HALF, HALF, axis=1)

    whole = np.arange(64)
    dx, dy = (whole // 8 - x) % 4, (whole // 2 - y) % 4
    da, db = jnp.where(core == 0, dx, dy), jnp.where(core == 0, dy, dx)
    met_at = ((((whole // 32) ^ zh) * 4 + db) * 4 + da) * 2 + ((whole % 2) ^ core)
    met_at = met_at.astype(jnp.int32)
    order = np.arange(64)
    oz, ob, oa, oc = order // 32, (order // 8) % 4, (order // 2) % 4, order % 2

    def folded_at(side):
        ox, oy = jnp.where(side == 0, oa, ob), jnp.where(side == 0, ob, oa)
        block = (((oz ^ zh) * 4 + (ox + x) % 4) * 4 + (oy + y) % 4) * 2 + (oc ^ side)
        quarter = block // 16
        return ((((quarter % 2) ^ (mp % 2)) * 2 + quarter // 2) * 16) + block % 16


    flipped = tokens.T
    crossed_x = send(flipped, crossed(1))
    probs, masked = make_masked(logits, gumbel, weight)
    block = in_vmem(
        stack_kernel, [shape16(96)],
        half(masked, core), send(half(masked, 1 - core), SIBLING), after=(crossed_x,),
    )[0]
    blocks = [block, send(block, PARTNER)]

    def start_of(dz, db):
        return (dz * 4 + db) * 384

    def spread_a(mine):
        return [mine, send(mine, A_DOWN), send(mine, A_TWO), send(mine, A_UP)]

    def kept(dz, up, down, after):
        own, one, two, three = in_vmem(
            functools.partial(keep_kernel, start_of(dz, 0)),
            [jax.ShapeDtypeStruct((96, HALF), F32)] + [shape16(96)] * 3, acts, cot, up, down,
            after=after,
        )
        return own, send(one, A_UP), send(two, A_TWO), send(three, A_DOWN)

    cot = jnp.concatenate(
        [half(cotangent, core), send(half(cotangent, 1 - core), SIBLING)], axis=0
    )
    line0 = in_vmem(
        stack_kernel, [shape16(384)], *spread_a(blocks[0]), after=(blocks[1], cot)
    )[0]
    near0, far0 = send(line0, B_DOWN), send(line0, B_UP)
    own = in_vmem(
        stack_kernel, [jax.ShapeDtypeStruct((1536, 128), BF16)], flipped, crossed_x, after=(line0,)
    )[0]
    line1 = in_vmem(stack_kernel, [shape16(384)], *spread_a(blocks[1]))[0]
    near1, far1 = send(line1, B_DOWN), send(line1, B_UP)
    whole_x = in_vmem(
        stack_kernel, [jax.ShapeDtypeStruct((3072, 128), BF16)],
        own, send(own, crossed(2)), after=(line1,),
    )[0]

    came = jnp.concatenate([(mp ^ r) * 16 + np.arange(16) for r in range(4)])
    acts = meet(met_at[came], whole_x, send(whole_x, SIBLING))
    up2, down2 = in_vmem(
        functools.partial(second_kernel, start_of(1, 2)),
        [shape16(384)] * 2, acts, cot, near0, far0, after=(line1,),
    )
    high0, low0 = send(up2, B_UP), send(down2, B_DOWN)
    result, *grad_a = products(
        acts, cot, None,
        [
            (start_of(0, 0), 0, 384, line0),
            (start_of(0, 1), 0, 384, near0),
            (start_of(0, 3), 0, 384, far0),
        ],
        (up2,),
    )
    up3, down3 = in_vmem(
        functools.partial(second_kernel, start_of(0, 2)),
        [shape16(384)] * 2, acts, cot, near1, far1, after=(result,),
    )
    result, *grad_c = products(
        acts, cot, result,
        [
            (start_of(1, 0), 0, 384, line1),
            (start_of(1, 1), 0, 384, near1),
            (start_of(1, 3), 0, 384, far1),
        ],
        (up3,),
    )
    high1, low1 = send(up3, B_UP), send(down3, B_DOWN)
    up4, down4 = in_vmem(
        functools.partial(third_kernel, start_of(1, 1), start_of(1, 3)),
        [shape16(384)] * 2, acts, cot, high0, low0, after=(result,),
    )
    result, *grad_b = products(
        acts, cot, result,
        [(start_of(0, 2), 0, 192, low0), (start_of(0, 2) + 192, 0, 192, high0)],
        (up4,), LIGHT, joined=grad_a,
    )
    up4, down4 = send(up4, B_UP), send(down4, B_DOWN)
    up5, down5 = in_vmem(
        functools.partial(third_kernel, start_of(0, 1), start_of(0, 3)),
        [shape16(384)] * 2, acts, cot, high1, low1,
        after=(grad_b[0],),
    )
    result, *grad_d = products(
        acts, cot, result,
        [(start_of(1, 2), 0, 192, low1), (start_of(1, 2) + 192, 0, 192, high1)],
        (up4,), LIGHT, BF16, grad_c,
    )
    up5, down5 = send(up5, B_UP), send(down5, B_DOWN)
    keep, give = fold(
        fold_kernel, jnp.concatenate([folded_at(core), folded_at(1 - core)]), 1536,
        grad_b[0], grad_d[0], send(grad_b[1], SIBLING), send(grad_d[1], SIBLING),
        scratch=[pltpu.VMEM((3072, 128), F32)],
    )
    own_part, give = fold(
        half_kernel, jnp.reshape(mp // 2, (1,)), 768, keep, send(give, crossed(1))
    )
    total = own_part + send(give, crossed(2))

    sums = in_vmem(sum_kernel, [shape16(96)], *kept(1, up4, down4, ()))
    sums += in_vmem(
        sum_kernel,
        [jax.ShapeDtypeStruct((96, HALF), F32)], *kept(0, up5, down5, (sums[0],)),
        after=(own_part,),
    )
    wsum = sums[1] + send(sums[0], PARTNER).astype(F32)
    other = send(wsum[ROWS:], SIBLING)
    wgrad = jnp.where(
        core == 0,
        jnp.concatenate([wsum[:ROWS], other], axis=1),
        jnp.concatenate([other, wsum[:ROWS]], axis=1),
    )
    new_logits, new_one, new_two = adam(wgrad, weight, probs, logits, moment_one, moment_two)

    other = send(result[128:], SIBLING)
    output = jnp.where(
        core == 0,
        jnp.concatenate([result[:128], other], axis=1),
        jnp.concatenate([other, result[:128]], axis=1),
    )

    input_grad = total.astype(BF16).T
    return (output, input_grad, new_logits, new_one, new_two)


def solution(mesh):
    placed = (
        P("dp", "mp"),
        P("dp", "mp"),
        P(None, "dp", "mp"),
        P(None, "dp", "mp"),
        P("dp", "mp"),
        P(None, "dp", "mp"),
        P(None, "dp", "mp"),
    )
    return jax.shard_map(
        local,
        mesh=mesh,
        in_specs=placed,
        out_specs=(
            P("dp", "mp"),
            P("dp", "mp"),
            P(None, "dp", "mp"),
            P(None, "dp", "mp"),
            P(None, "dp", "mp"),
        ),
        check_vma=False,
    )
```

```python
import functools

import jax
import jax.numpy as jnp
import numpy as np
from jax import lax
from jax.experimental import pallas as pl
from jax.experimental.pallas import tpu as pltpu
from jax.sharding import PartitionSpec as P

beta_one = 0.9
beta_two = 0.999
adam_eps = 1e-08
decay = 0.01
rate = 0.1
adam_step = 10.0

F32 = jnp.float32
BF16 = jnp.bfloat16
AXES = ("dp", "mp")
SIZES = (2, 4, 4, 2, 4)
PAIRS = tuple((i, j) for i in range(4) for j in range(i + 1, 4))
ROWS = 48
HALF = 1536
WIDE = 512
TILE = 512
MIB = 1 << 20
IN_VMEM = pl.BlockSpec(memory_space=pltpu.VMEM)
HEAVY = pl.CostEstimate(flops=20000000000, bytes_accessed=1, transcendentals=0)
LIGHT = pl.CostEstimate(flops=0, bytes_accessed=1, transcendentals=0)


def pairs_of(target):
    found = []
    for here in np.ndindex(*SIZES):
        there = tuple(a % b for a, b in zip(target(*here), SIZES))
        found.append(
            (int(np.ravel_multi_index(here, SIZES)), int(np.ravel_multi_index(there, SIZES)))
        )
    return found


def step_a(by):
    return pairs_of(
        lambda z, x, y, c, m: (z, x + by, y, c, m) if c == 0 else (z, x, y + by, c, m)
    )


def step_b(by):
    return pairs_of(
        lambda z, x, y, c, m: (z, x, y + by, c, m) if c == 0 else (z, x + by, y, c, m)
    )


SIBLING = pairs_of(lambda z, x, y, c, m: (z, x, y, c + 1, m))
PARTNER = pairs_of(lambda z, x, y, c, m: (z + 1, x, y, c, m))
A_UP, A_DOWN, A_TWO = step_a(1), step_a(-1), step_a(2)
B_UP, B_DOWN = step_b(1), step_b(-1)


def around(by):
    return pairs_of(lambda z, x, y, c, m: (z, x, y, c, m + by))


def crossed(by):
    return pairs_of(lambda z, x, y, c, m: (z, x, y, c, m ^ by))


def send(value, pairs):
    return lax.ppermute(value, AXES, pairs)


def dot(a, b, dims):
    return lax.dot_general(a, b, (dims, ((), ())), preferred_element_type=F32)


def mask_kernel(logits, gumbel, weight, probs, masked, spread):
    scores = [logits[p] + gumbel[p].astype(F32) for p in range(6)]
    top = scores[0]
    for p in range(1, 6):
        top = jnp.maximum(top, scores[p])
    exps = [jnp.exp(s - top) for s in scores]
    total = exps[0]
    for p in range(1, 6):
        total = total + exps[p]
    share = [e / total for e in exps]
    for p in range(6):
        probs[p] = share[p]
    for slot in range(4):
        kept = [share[p] for p in range(6) if slot in PAIRS[p]]
        mask = kept[0] + kept[1] + kept[2]
        for j in range(WIDE // 128):
            at = j * 128
            spread[pl.ds(j * ROWS + slot, 12, stride=4), :] = mask[:, at : at + 128]
    for j in range(WIDE // 128):
        at = j * 128
        part = weight[:, at : at + 128].astype(F32) * spread[j * ROWS : (j + 1) * ROWS, :]
        masked[:, at : at + 128] = part.astype(BF16)


def make_masked(logits, gumbel, weight):
    cols = weight.shape[1]
    wide = WIDE
    three = pl.BlockSpec((6, 12, wide), lambda i: (0, 0, i))
    two = pl.BlockSpec((ROWS, wide), lambda i: (0, i))
    return pl.pallas_call(
        mask_kernel,
        grid=(cols // wide,),
        in_specs=[three, three, two],
        out_specs=[three, two],
        out_shape=[
            jax.ShapeDtypeStruct((6, 12, cols), F32),
            jax.ShapeDtypeStruct((ROWS, cols), BF16),
        ],
        scratch_shapes=[pltpu.VMEM((wide // 128 * ROWS, 128), F32)],
        compiler_params=pltpu.CompilerParams(vmem_limit_bytes=16 * MIB),
        cost_estimate=LIGHT,
    )(logits, gumbel, weight)


def adam_kernel(wgrad, weight, probs, logits, one, two, new_logits, new_one, new_two, spread):
    for j in range(WIDE // 128):
        at = j * 128
        spread[j * ROWS : (j + 1) * ROWS, :] = (
            weight[:, at : at + 128].astype(F32) * wgrad[:, at : at + 128]
        )
    slots = [
        jnp.concatenate(
            [spread[pl.ds(j * ROWS + slot, 12, stride=4), :] for j in range(WIDE // 128)], axis=1
        )
        for slot in range(4)
    ]
    pgrad = [slots[i] + slots[j] for i, j in PAIRS]
    share = [probs[p] for p in range(6)]
    mean = share[0] * pgrad[0]
    for p in range(1, 6):
        mean = mean + share[p] * pgrad[p]
    for p in range(6):
        lgrad = share[p] * (pgrad[p] - mean)
        first = beta_one * one[p] + (1.0 - beta_one) * lgrad
        second = beta_two * two[p] + (1.0 - beta_two) * lgrad * lgrad
        new_one[p] = first
        new_two[p] = second
        first_hat = first / (1.0 - beta_one**adam_step)
        second_hat = second / (1.0 - beta_two**adam_step)
        old = logits[p]
        new_logits[p] = old - rate * (first_hat / (jnp.sqrt(second_hat) + adam_eps) + decay * old)


def adam(wgrad, weight, probs, logits, one, two):
    cols = weight.shape[1]
    wide = WIDE
    three = pl.BlockSpec((6, 12, wide), lambda i: (0, 0, i))
    flat = pl.BlockSpec((ROWS, wide), lambda i: (0, i))
    out = jax.ShapeDtypeStruct((6, 12, cols), F32)
    return pl.pallas_call(
        adam_kernel,
        grid=(cols // wide,),
        in_specs=[flat, flat, three, three, three, three],
        out_specs=[three, three, three],
        out_shape=[out, out, out],
        scratch_shapes=[pltpu.VMEM((wide // 128 * ROWS, 128), F32)],
        compiler_params=pltpu.CompilerParams(vmem_limit_bytes=16 * MIB),
        cost_estimate=LIGHT,
    )(wgrad, weight, probs, logits, one, two)


def meet_kernel(place, mine, other, out):
    for i in range(64):
        at = pl.multiple_of(place[i] * ROWS, ROWS)
        out[pl.ds(at, ROWS), :128] = mine[i * ROWS : (i + 1) * ROWS, :]
        out[pl.ds(at, ROWS), 128:] = other[i * ROWS : (i + 1) * ROWS, :]


def meet(place, mine, other):
    return pl.pallas_call(
        meet_kernel,
        in_specs=[pl.BlockSpec(memory_space=pltpu.SMEM)] + [IN_VMEM] * 2,
        out_specs=IN_VMEM,
        out_shape=jax.ShapeDtypeStruct((3072, 256), BF16),
        compiler_params=pltpu.CompilerParams(vmem_limit_bytes=16 * MIB),
        cost_estimate=LIGHT,
    )(place, mine, other)


BLOCKS = (
    (*range(0, 16), *range(24, 32), *range(16, 24)),
    (*range(32, 48), *range(56, 64), *range(48, 56)),
)


def fold_kernel(place, *refs):
    keep, give, total = refs[-3:]
    for group, blocks in enumerate(BLOCKS):
        for i, block in enumerate(blocks):
            at = pl.multiple_of(place[block] * ROWS, ROWS)
            total[pl.ds(at, ROWS), :] = refs[group][i * ROWS : (i + 1) * ROWS, :]
    for group, blocks in enumerate(BLOCKS):
        for i, block in enumerate(blocks):
            at = pl.multiple_of(place[64 + block] * ROWS, ROWS)
            rows = pl.ds(at, ROWS)
            total[rows, :] = total[rows, :] + refs[2 + group][i * ROWS : (i + 1) * ROWS, :]
    keep[...] = total[:1536, :]
    give[...] = total[1536:, :]


def half_kernel(place, mine, other, keep, give):
    at = pl.multiple_of(place[0] * 768, 768)
    keep[...] = mine[pl.ds(at, 768), :] + other[pl.ds(at, 768), :]
    at = pl.multiple_of((1 - place[0]) * 768, 768)
    give[...] = mine[pl.ds(at, 768), :] + other[pl.ds(at, 768), :]


def fold(kernel, place, rows, *parts, scratch=()):
    out = jax.ShapeDtypeStruct((rows, 128), F32)
    return pl.pallas_call(
        kernel,
        in_specs=[pl.BlockSpec(memory_space=pltpu.SMEM)] + [IN_VMEM] * len(parts),
        out_specs=[IN_VMEM] * 2,
        out_shape=[out, out],
        scratch_shapes=scratch,
        compiler_params=pltpu.CompilerParams(vmem_limit_bytes=16 * MIB),
        cost_estimate=LIGHT,
    )(place.astype(jnp.int32), *parts)


def share(acts, cot, start, count, at):
    return dot(acts[start : start + count, :], cot[:, at : at + TILE], ((1,), (0,)))


def stack_kernel(*refs):
    out, at = refs[-1], 0
    for ref in refs[:-1]:
        out[at : at + ref.shape[0], :] = ref[...].astype(out.dtype)
        at += ref.shape[0]


def lead(acts, cot, start, base, up, down):
    for at in range(0, HALF, TILE):
        cols = slice(at, at + TILE)
        up[base : base + 192, cols] = share(acts, cot, start, 192, at).astype(BF16)
        down[base : base + 192, cols] = share(acts, cot, start + 192, 192, at).astype(BF16)


def follow(acts, cot, start_up, start_down, low, high, base, up, down):
    for at in range(0, HALF, TILE):
        cols = slice(at, at + TILE)
        got = share(acts, cot, start_up, 192, at) + low[base : base + 192, cols].astype(F32)
        up[:192, cols] = got.astype(BF16)
        up[192:384, cols] = share(acts, cot, start_up + 192, 192, at).astype(BF16)
        down[:192, cols] = share(acts, cot, start_down, 192, at).astype(BF16)
        got = share(acts, cot, start_down + 192, 192, at) + high[base : base + 192, cols].astype(F32)
        down[192:384, cols] = got.astype(BF16)


def second_kernel(start, acts, cot, near, far, up, down):
    up[:192, :] = far[192:384, :]
    down[:192, :] = near[:192, :]
    lead(acts, cot, start, 192, up, down)


def third_kernel(start_up, start_down, acts, cot, low, high, up, down):
    follow(acts, cot, start_up, start_down, low, high, 192, up, down)


def sum_kernel(own, one, two, three, out):
    total = own[...] + one[...].astype(F32) + two[...].astype(F32) + three[...].astype(F32)
    out[...] = total.astype(out.dtype)


def keep_kernel(start, acts, cot, up, down, own, *others):
    for at in range(0, HALF, TILE):
        cols = slice(at, at + TILE)
        for i in range(4):
            rows = slice(i * 96, i * 96 + 96)
            got = share(acts, cot, start + i * 96, 96, at)
            got = got + up[rows, cols].astype(F32) + down[rows, cols].astype(F32)
            if i == 0:
                own[:, cols] = got
            else:
                others[i - 1][:, cols] = got.astype(BF16)


def in_vmem(kernel, out_shape, *args, after=(), cost=LIGHT):
    if after:
        inner, count, kept = kernel, len(args), len(args) + len(after)

        def kernel(*refs):
            inner(*refs[:count], *refs[kept:])

        args = args + tuple(after)
    return pl.pallas_call(
        kernel,
        in_specs=[IN_VMEM] * len(args),
        out_specs=[IN_VMEM] * len(out_shape),
        out_shape=out_shape,
        compiler_params=pltpu.CompilerParams(vmem_limit_bytes=24 * MIB),
        cost_estimate=cost,
    )(*args)


def shape16(rows):
    return jax.ShapeDtypeStruct((rows, HALF), BF16)


def product_kernel(spans, first, joined, acts, cot, *refs):
    size = len(spans)
    before = None if first else refs[0]
    refs = refs if first else refs[1:]
    pieces, (result, mine, theirs) = refs[:size], refs[-3:]
    for at in range(0, HALF, TILE):
        cols = slice(at, at + TILE)
        total = None if first else before[:, cols]
        for (start, skip, count), piece in zip(spans, pieces):
            rows = piece[skip : skip + count, cols]
            term = dot(acts[start : start + count, :], rows, ((0,), (0,)))
            total = term if total is None else total + term
        result[:, cols] = total.astype(result.dtype)
    at = 0
    if joined:
        at = refs[size].shape[0]
        mine[:at, :] = refs[size][...]
        theirs[:at, :] = refs[size + 1][...]
    for (start, skip, count), piece in zip(spans, pieces):
        grad = dot(piece[skip : skip + count, :], cot[...], ((1,), (1,)))
        mine[at : at + count, :] = grad[:, :128]
        theirs[at : at + count, :] = grad[:, 128:]
        at += count


def products(acts, cot, before, parts, after, cost=HEAVY, kind=F32, joined=()):
    first = before is None
    spans = [p[:3] for p in parts]
    rows = sum(p[2] for p in parts) + (joined[0].shape[0] if joined else 0)
    columns = jax.ShapeDtypeStruct((rows, 128), F32)
    shapes = [jax.ShapeDtypeStruct((256, HALF), kind), columns, columns]
    args = [acts, cot] + ([] if first else [before]) + [p[3] for p in parts] + list(joined)
    kernel = functools.partial(product_kernel, spans, first, bool(joined))
    return in_vmem(kernel, shapes, *args, after=after, cost=cost)


def local(tokens, weight, logits, gumbel, cotangent, moment_one, moment_two):
    dp = lax.axis_index("dp")
    mp = lax.axis_index("mp")
    core, y, x, zh = dp % 2, (dp // 2) % 4, (dp // 8) % 4, dp // 32

    def half(value, which):
        return lax.dynamic_slice_in_dim(value, which * HALF, HALF, axis=1)

    whole = np.arange(64)
    dx, dy = (whole // 8 - x) % 4, (whole // 2 - y) % 4
    da, db = jnp.where(core == 0, dx, dy), jnp.where(core == 0, dy, dx)
    met_at = ((((whole // 32) ^ zh) * 4 + db) * 4 + da) * 2 + ((whole % 2) ^ core)
    met_at = met_at.astype(jnp.int32)
    order = np.arange(64)
    oz, ob, oa, oc = order // 32, (order // 8) % 4, (order // 2) % 4, order % 2

    def folded_at(side):
        ox, oy = jnp.where(side == 0, oa, ob), jnp.where(side == 0, ob, oa)
        block = (((oz ^ zh) * 4 + (ox + x) % 4) * 4 + (oy + y) % 4) * 2 + (oc ^ side)
        quarter = block // 16
        return ((((quarter % 2) ^ (mp % 2)) * 2 + quarter // 2) * 16) + block % 16


    flipped = tokens.T
    crossed_x = send(flipped, crossed(1))
    probs, masked = make_masked(logits, gumbel, weight)
    block = in_vmem(
        stack_kernel, [shape16(96)],
        half(masked, core), send(half(masked, 1 - core), SIBLING), after=(crossed_x,),
    )[0]
    blocks = [block, send(block, PARTNER)]

    def start_of(dz, db):
        return (dz * 4 + db) * 384

    def spread_a(mine):
        return [mine, send(mine, A_DOWN), send(mine, A_TWO), send(mine, A_UP)]

    def kept(dz, up, down, after):
        own, one, two, three = in_vmem(
            functools.partial(keep_kernel, start_of(dz, 0)),
            [jax.ShapeDtypeStruct((96, HALF), F32)] + [shape16(96)] * 3, acts, cot, up, down,
            after=after,
        )
        return own, send(one, A_UP), send(two, A_TWO), send(three, A_DOWN)

    cot = jnp.concatenate(
        [half(cotangent, core), send(half(cotangent, 1 - core), SIBLING)], axis=0
    )
    line0 = in_vmem(
        stack_kernel, [shape16(384)], *spread_a(blocks[0]), after=(blocks[1], cot)
    )[0]
    near0, far0 = send(line0, B_DOWN), send(line0, B_UP)
    own = in_vmem(
        stack_kernel, [jax.ShapeDtypeStruct((1536, 128), BF16)], flipped, crossed_x, after=(line0,)
    )[0]
    line1 = in_vmem(stack_kernel, [shape16(384)], *spread_a(blocks[1]))[0]
    near1, far1 = send(line1, B_DOWN), send(line1, B_UP)
    whole_x = in_vmem(
        stack_kernel, [jax.ShapeDtypeStruct((3072, 128), BF16)],
        own, send(own, crossed(2)), after=(line1,),
    )[0]

    came = jnp.concatenate([(mp ^ r) * 16 + np.arange(16) for r in range(4)])
    acts = meet(met_at[came], whole_x, send(whole_x, SIBLING))
    up2, down2 = in_vmem(
        functools.partial(second_kernel, start_of(1, 2)),
        [shape16(384)] * 2, acts, cot, near0, far0, after=(line1,),
    )
    high0, low0 = send(up2, B_UP), send(down2, B_DOWN)
    result, *grad_a = products(
        acts, cot, None,
        [
            (start_of(0, 0), 0, 384, line0),
            (start_of(0, 1), 0, 384, near0),
            (start_of(0, 3), 0, 384, far0),
        ],
        (up2,),
    )
    up3, down3 = in_vmem(
        functools.partial(second_kernel, start_of(0, 2)),
        [shape16(384)] * 2, acts, cot, near1, far1, after=(result,),
    )
    result, *grad_c = products(
        acts, cot, result,
        [
            (start_of(1, 0), 0, 384, line1),
            (start_of(1, 1), 0, 384, near1),
            (start_of(1, 3), 0, 384, far1),
        ],
        (up3,),
    )
    high1, low1 = send(up3, B_UP), send(down3, B_DOWN)
    up4, down4 = in_vmem(
        functools.partial(third_kernel, start_of(1, 1), start_of(1, 3)),
        [shape16(384)] * 2, acts, cot, high0, low0, after=(result,),
    )
    result, *grad_b = products(
        acts, cot, result,
        [(start_of(0, 2), 0, 192, low0), (start_of(0, 2) + 192, 0, 192, high0)],
        (up4,), LIGHT, joined=grad_a,
    )
    up4, down4 = send(up4, B_UP), send(down4, B_DOWN)
    up5, down5 = in_vmem(
        functools.partial(third_kernel, start_of(0, 1), start_of(0, 3)),
        [shape16(384)] * 2, acts, cot, high1, low1,
        after=(grad_b[0],),
    )
    result, *grad_d = products(
        acts, cot, result,
        [(start_of(1, 2), 0, 192, low1), (start_of(1, 2) + 192, 0, 192, high1)],
        (up4,), LIGHT, BF16, grad_c,
    )
    up5, down5 = send(up5, B_UP), send(down5, B_DOWN)
    keep, give = fold(
        fold_kernel, jnp.concatenate([folded_at(core), folded_at(1 - core)]), 1536,
        grad_b[0], grad_d[0], send(grad_b[1], SIBLING), send(grad_d[1], SIBLING),
        scratch=[pltpu.VMEM((3072, 128), F32)],
    )
    own_part, give = fold(
        half_kernel, jnp.reshape(mp // 2, (1,)), 768, keep, send(give, crossed(1))
    )
    total = own_part + send(give, crossed(2))

    sums = in_vmem(sum_kernel, [shape16(96)], *kept(1, up4, down4, ()))
    sums += in_vmem(
        sum_kernel,
        [jax.ShapeDtypeStruct((96, HALF), F32)], *kept(0, up5, down5, (sums[0],)),
        after=(own_part,),
    )
    wsum = sums[1] + send(sums[0], PARTNER).astype(F32)
    swapped = send(
        in_vmem(
            stack_kernel, [jax.ShapeDtypeStruct((128 + ROWS, HALF), F32)],
            result[128:], wsum[ROWS:],
        )[0],
        SIBLING,
    )
    other = swapped[128:]
    wgrad = jnp.where(
        core == 0,
        jnp.concatenate([wsum[:ROWS], other], axis=1),
        jnp.concatenate([other, wsum[:ROWS]], axis=1),
    )
    new_logits, new_one, new_two = adam(wgrad, weight, probs, logits, moment_one, moment_two)

    other = swapped[:128].astype(BF16)
    output = jnp.where(
        core == 0,
        jnp.concatenate([result[:128], other], axis=1),
        jnp.concatenate([other, result[:128]], axis=1),
    )

    input_grad = total.astype(BF16).T
    return (output, input_grad, new_logits, new_one, new_two)


def solution(mesh):
    placed = (
        P("dp", "mp"),
        P("dp", "mp"),
        P(None, "dp", "mp"),
        P(None, "dp", "mp"),
        P("dp", "mp"),
        P(None, "dp", "mp"),
        P(None, "dp", "mp"),
    )
    return jax.shard_map(
        local,
        mesh=mesh,
        in_specs=placed,
        out_specs=(
            P("dp", "mp"),
            P("dp", "mp"),
            P(None, "dp", "mp"),
            P(None, "dp", "mp"),
            P(None, "dp", "mp"),
        ),
        check_vma=False,
    )
```
